128 devices in a mesh: dp: 16 (over y_lo, z, core), cp: 8 (over x, y_hi).
Axes of the slice: x: 4, y: 4 (y_hi: 2, y_lo: 2; y = y_hi * 2 + y_lo), z: 4, core: 2. Of those that a mesh axis runs over, the one named last changes fastest.
Arguments:
- queries: bfloat16 [16384, 3072], P(('dp', 'cp')), may hold values from -48 to 48
- key_heads: bfloat16 [16384, 512], P(('dp', 'cp')), may hold values from -6 to 6
- value_heads: bfloat16 [16384, 512], P(('dp', 'cp')), may hold values from -6 to 6
- segment_ids: int32 [16, 1024], P('dp', 'cp'), may hold values from 0 to 1, never falling along the last dimension, each value on 1 to 768 neighbouring positions
- out_weight: bfloat16 [3072, 3072], P('dp', 'cp'), may hold values from -0.109375 to 0.109375
- grad_out: bfloat16 [16384, 3072], P('dp', 'cp'), may hold values from -6 to 6
Outputs:
- output: bfloat16 [16384, 3072], P('dp', 'cp')
- grad_queries: bfloat16 [16384, 3072], P(('dp', 'cp'))
- grad_keys: bfloat16 [16384, 512], P(('dp', 'cp'))
- grad_values: bfloat16 [16384, 512], P(('dp', 'cp'))
- grad_weight: float32 [3072, 3072], P('dp', 'cp')
The draws below stay inside these ranges and needn't reach their ends.
Inputs may be any that keep to these rules, and one draw needn't show every extreme that they name: `segment_ids`: document numbers of a group never fall; a document holds at most 768 positions.
All inputs are finite; a program needn't handle non-finite values.
Results may differ from the reference program's by a relative error of at most 0.023.
Values may be sent and summed in bfloat16 or wider, within the bound.
No kernel may reach another device: no remote copies, remote signals or barrier semaphores. Data moves between devices by JAX's collectives and lax.ppermute only.
A program may use at most 128 MiB of HBM per device.

```python
import math
import jax
import jax.numpy as jnp
import numpy as np
from jax import lax

HQ = 24
HK = 4
HD = 128
DOUT = 3072
SEGS = 2
QW = 3072
KW = 512
GROUP = 1024
TOKENS = 16384
N_DP = 16


def paired_keys(key):
    base_key = jax.random.fold_in(key, 101)
    drawn = jax.random.normal(base_key, (TOKENS, KW), jnp.float32)
    return jnp.clip(drawn, -6.0, 6.0)


def draw_key_heads(key, part):
    result = paired_keys(key)
    return result.astype(jnp.bfloat16)


def draw_queries(key, part):
    key = jax.random.fold_in(key, 5)
    result = jax.random.normal(key, (TOKENS, QW), jnp.float32)
    return jnp.clip(result, -48.0, 48.0).astype(jnp.bfloat16)


def block_levels(key, shape, cuts, smallest, top_value):
    factor_of = 1.0
    for dim, parts in cuts:
        draws = jax.random.uniform(jax.random.fold_in(jax.random.fold_in(key, 6), dim), (parts,), jnp.float32, smallest / len(cuts), top_value / len(cuts))
        factor_of = factor_of * jnp.repeat(jnp.exp(draws), shape[dim] // parts).reshape((-1,) + (1,) * (len(shape) - 1 - dim))
    return factor_of


def profile(number_of, total, bound, slope):
    weights = [(1 << 20) // math.isqrt(grade ** slope) + 1 for grade in range(2, number_of + 1)]
    rest, given = total - bound - (number_of - 1), [1] * (number_of - 1)
    while rest > 0:
        free = [i for i in range(number_of - 1) if given[i] < bound]
        whole, remaining = sum([weights[i] for i in free]), rest
        for i in free:
            extra = min(bound - given[i], max(1, remaining * weights[i] // whole), rest)
            given[i] = given[i] + extra
            rest = rest - extra
    return np.array([bound] + given)


def ragged_sizes(key, number_of, total, bound, slope):
    if number_of == 2:
        one = jax.random.randint(key, (), max(1, total - bound), min(bound, total - 1) + 1)
        return jnp.stack([one, total - one])
    tallies = jnp.asarray(profile(number_of, total, bound, slope), jnp.int32)
    pairs = (number_of - 1) // 2
    donor, receiver = tallies[1:1 + 2 * pairs:2], tallies[2:2 + 2 * pairs:2]
    room = jnp.minimum(donor - 1, bound - receiver)
    moved = jax.random.randint(jax.random.fold_in(key, 1), (pairs,), 0, 1 << 20) % (room + 1)
    tallies = tallies.at[1:1 + 2 * pairs:2].set(donor - moved).at[2:2 + 2 * pairs:2].set(receiver + moved)
    return tallies[jax.random.permutation(jax.random.fold_in(key, 2), number_of)]


def scatter_about(key, dims, width, reach, split=(), held_as=jnp.bfloat16):
    loudness = block_levels(key, dims, split, -0.22, 0.18) if split else 1.0
    values = jax.random.normal(key, dims, jnp.float32) * width * loudness
    return jnp.minimum(jnp.maximum(values, -reach), reach).astype(held_as)


def setup_inputs(seed: int = 0) -> dict:
    seeds = jax.random.split(jax.random.key(seed), 7)
    queries = draw_queries(jax.random.fold_in(seeds[6], 71), 0)
    key_heads = draw_key_heads(jax.random.fold_in(seeds[6], 71), 0)
    value_heads = scatter_about(seeds[2], (TOKENS, KW), 1.0, 6.0, ((0, 128),))
    segment_ids = jax.vmap(lambda own: jnp.searchsorted(jnp.cumsum(ragged_sizes(own, SEGS, GROUP, GROUP * 3 // 4, 2)), jnp.arange(GROUP), side="right"))(jax.random.split(seeds[3], N_DP)).reshape((N_DP, GROUP)).astype(jnp.int32)
    out_weight = scatter_about(seeds[4], (QW, DOUT), QW ** -0.5, 0.109375, ((0, 16), (1, 8)))
    grad_out = scatter_about(seeds[5], (TOKENS, DOUT), 1.0, 6.0, ((0, 16), (1, 8)))
    return {"queries": queries, "key_heads": key_heads, "value_heads": value_heads, "segment_ids": segment_ids, "out_weight": out_weight, "grad_out": grad_out}


def to_bf16(values_f32):
    return lax.optimization_barrier(values_f32.astype(jnp.bfloat16)).astype(jnp.float32)

def attend_group(group_queries, group_keys, group_values, group_segments, group_grad, weight):
    rows = group_queries.shape[0]
    head_share = HQ // HK
    score_scale = 1.0 / math.sqrt(HD)
    query_tiles = group_queries.astype(jnp.float32).reshape(rows, HK, head_share, HD)
    key_tiles = group_keys.astype(jnp.float32).reshape(rows, HK, HD)
    value_tiles = group_values.astype(jnp.float32).reshape(rows, HK, HD)
    logits = jnp.einsum('qhrd,khd->hrqk', query_tiles, key_tiles) * score_scale
    position = jnp.arange(rows, dtype=jnp.int32)
    allowed = (group_segments[:, None] == group_segments[None, :]) & (position[None, :] <= position[:, None])
    masked = jnp.where(allowed, logits, -1e+30)
    row_peak = lax.optimization_barrier(jnp.max(masked, axis=-1, keepdims=True))
    weights = jnp.where(allowed, jnp.exp(masked - row_peak), 0.0)
    probability = weights / lax.optimization_barrier(jnp.sum(weights, axis=-1, keepdims=True))
    rounded_prob = to_bf16(probability)
    attended = jnp.einsum('hrqk,khd->qhrd', rounded_prob, value_tiles).astype(jnp.bfloat16).reshape(rows, QW)
    output = jnp.dot(attended, weight, preferred_element_type=jnp.float32).astype(jnp.bfloat16)
    grad_attended = lax.dot_general(group_grad, weight, (((1,), (1,)), ((), ())), preferred_element_type=jnp.float32).astype(jnp.bfloat16)
    weight_partial = lax.dot_general(attended, group_grad, (((0,), (0,)), ((), ())), preferred_element_type=jnp.float32)
    grad_tiles = grad_attended.astype(jnp.float32).reshape(rows, HK, head_share, HD)
    grad_prob = jnp.einsum('qhrd,khd->hrqk', grad_tiles, value_tiles)
    delta = lax.optimization_barrier(jnp.sum(probability * grad_prob, axis=-1, keepdims=True))
    grad_logit = to_bf16(probability * (grad_prob - delta))
    grad_queries = (jnp.einsum('hrqk,khd->qhrd', grad_logit, key_tiles) * score_scale).astype(jnp.bfloat16).reshape(rows, QW)
    grad_keys = (jnp.einsum('hrqk,qhrd->khd', grad_logit, query_tiles) * score_scale).astype(jnp.bfloat16).reshape(rows, KW)
    grad_values = jnp.einsum('hrqk,qhrd->khd', rounded_prob, grad_tiles).astype(jnp.bfloat16).reshape(rows, KW)
    return (output, grad_queries, grad_keys, grad_values, weight_partial)

def reference(queries, key_heads, value_heads, segment_ids, out_weight, grad_out):
    stacked = (queries.reshape(N_DP, GROUP, QW), key_heads.reshape(N_DP, GROUP, KW), value_heads.reshape(N_DP, GROUP, KW), segment_ids, grad_out.reshape(N_DP, GROUP, DOUT))

    def one_step(weight_sum, group_inputs):
        output, grad_queries, grad_keys, grad_values, weight_partial = attend_group(group_inputs[0], group_inputs[1], group_inputs[2], group_inputs[3], group_inputs[4], out_weight)
        return (weight_sum + weight_partial, (output, grad_queries, grad_keys, grad_values))
    weight_sum, results = lax.scan(one_step, jnp.zeros((QW, DOUT), jnp.float32), stacked)
    output = results[0].reshape(TOKENS, DOUT)
    grad_queries = results[1].reshape(TOKENS, QW)
    grad_keys = results[2].reshape(TOKENS, KW)
    grad_values = results[3].reshape(TOKENS, KW)
    return (output, grad_queries, grad_keys, grad_values, weight_sum)
```

```python
import math

import jax
import jax.numpy as jnp
from jax import lax
from jax.experimental import pallas as pl
from jax.experimental.pallas import tpu as pltpu
from jax.sharding import PartitionSpec as P


NX = 4
GROUP = 1024
HD = 128
HEADS = 3
FEAT = 384
ROWS = 128
QB = 256
SEG_ROWS = 16
PACK = 5 * ROWS + SEG_ROWS
SHIFTS = [(dx, dh) for dx in range(NX) for dh in range(2)]
SCALE = 1.0 / math.sqrt(HD)
EXP2_SCALE = SCALE * math.log2(math.e)
F32 = jnp.float32
BF16 = jnp.bfloat16
VMEM_LIMIT = 48 * 1024 * 1024


def cp_pairs(dx, dh):
    return [(x * 2 + h, ((x + dx) % NX) * 2 + (h ^ dh)) for x in range(NX) for h in range(2)]


def z_pairs(dz):
    return [
        (y * 8 + z * 2 + c, y * 8 + ((z + dz) % 4) * 2 + c)
        for y in range(2)
        for z in range(4)
        for c in range(2)
    ]


def core_pairs():
    return [(d, d ^ 1) for d in range(16)]


def y_pairs(moves):
    pairs = []
    for src, dst in moves:
        for r in range(8):
            for x in range(NX):
                pairs.append(
                    (
                        ((src % 2) * 8 + r) * 8 + x * 2 + src // 2,
                        ((dst % 2) * 8 + r) * 8 + x * 2 + dst // 2,
                    )
                )
    return pairs


Y_SWAP = y_pairs([(1, 2), (2, 1)])
Y_CYCLE_IN = y_pairs([(0, 1), (2, 0), (3, 2), (1, 3)])
Y_CYCLE_OUT = y_pairs([(1, 0), (0, 2), (2, 3), (3, 1)])


def dot_nt(a, b):
    return lax.dot_general(a, b, (((1,), (1,)), ((), ())), preferred_element_type=F32)


def dot_nn(a, b):
    return lax.dot_general(a, b, (((1,), (0,)), ((), ())), preferred_element_type=F32)


def dot_tn(a, b):
    return lax.dot_general(a, b, (((0,), (0,)), ((), ())), preferred_element_type=F32)


def call(kernel, name, meta, operands, outs, scratch=(), flops=0, transcendentals=0):
    moved = sum(math.prod(o.shape) * o.dtype.itemsize for o in list(operands) + list(outs))
    return pl.pallas_call(
        kernel,
        name=name,
        out_shape=tuple(outs),
        in_specs=[pl.BlockSpec(memory_space=pltpu.SMEM)]
        + [pl.BlockSpec(memory_space=pltpu.VMEM)] * len(operands),
        out_specs=tuple(pl.BlockSpec(memory_space=pltpu.VMEM) for _ in outs),
        scratch_shapes=list(scratch),
        compiler_params=pltpu.CompilerParams(vmem_limit_bytes=VMEM_LIMIT),
        cost_estimate=pl.CostEstimate(
            flops=flops, bytes_accessed=moved, transcendentals=transcendentals
        ),
    )(meta, *operands)


def shaped(shape, dtype):
    return jax.ShapeDtypeStruct(shape, dtype)


def pack_kernel(meta, q_ref, k_ref, v_ref, seg_ref, *out_refs):
    x, h = meta[0], meta[1]
    seg = jnp.broadcast_to(seg_ref[...].astype(F32), (SEG_ROWS, ROWS)).astype(BF16)
    for (dx, dh), out in zip(SHIFTS, out_refs):
        to_x = lax.rem(x + dx, NX)
        to_h = h if dh == 0 else 1 - h
        q_off = pl.multiple_of(to_h * (NX * FEAT) + to_x * FEAT, 128)
        kv_off = pl.multiple_of((to_h * 2 + to_x // 2) * HD, 128)
        for head in range(HEADS):
            out[pl.ds(head * ROWS, ROWS), :] = q_ref[:, pl.ds(pl.multiple_of(q_off + head * HD, 128), HD)]
        out[pl.ds(3 * ROWS, ROWS), :] = k_ref[:, pl.ds(kv_off, HD)]
        out[pl.ds(4 * ROWS, ROWS), :] = v_ref[:, pl.ds(kv_off, HD)]
        out[pl.ds(5 * ROWS, SEG_ROWS), :] = seg


def transposed_scores(k, q, first, qb):
    scores = dot_nt(k, q)
    key_pos = lax.broadcasted_iota(jnp.int32, scores.shape, 0)
    query_pos = lax.broadcasted_iota(jnp.int32, scores.shape, 1) + qb * QB
    return jnp.where((key_pos <= query_pos) & (key_pos >= first), scores * EXP2_SCALE, -1e30)


def forward_kernel(meta, *refs):
    blocks, (att_ref, q_ref, kv_ref, stat_ref, vt_ref) = refs[:8], refs[8:]
    x, h = meta[0], meta[1]
    seg_sum = jnp.zeros((1, ROWS), F32)
    for (dx, dh), block in zip(SHIFTS, blocks):
        from_x = lax.rem(x - dx + NX, NX)
        from_h = h if dh == 0 else 1 - h
        row = pl.multiple_of((from_x * 2 + from_h) * ROWS, ROWS)
        for head in range(HEADS):
            q_ref[head, pl.ds(row, ROWS), :] = block[pl.ds(head * ROWS, ROWS), :]
        kv_ref[0, pl.ds(row, ROWS), :] = block[pl.ds(3 * ROWS, ROWS), :]
        kv_ref[1, pl.ds(row, ROWS), :] = block[pl.ds(4 * ROWS, ROWS), :]
        seg_sum = seg_sum + block[pl.ds(5 * ROWS, SEG_ROWS), :].astype(F32)[0:1]
    second = jnp.sum(seg_sum, axis=1, keepdims=True)
    boundary = (GROUP - second).astype(jnp.int32)
    position = lax.broadcasted_iota(jnp.int32, (1, GROUP), 1)
    first = jnp.where(position >= boundary, boundary, 0)
    stat_ref[...] = jnp.zeros_like(stat_ref)
    stat_ref[3:4, :] = first.astype(F32)
    vt_ref[...] = kv_ref[1].astype(F32).T.astype(BF16)
    for qb in range(GROUP // QB):
        keys = (qb + 1) * QB
        rows = pl.ds(qb * QB, QB)
        for head in range(HEADS):
            scores = transposed_scores(
                kv_ref[0, pl.ds(0, keys), :], q_ref[head, rows, :], first[:, qb * QB : keys], qb
            )
            peak = jnp.max(scores, axis=0, keepdims=True)
            weights = jnp.exp2(scores - peak)
            total = jnp.sum(weights, axis=0, keepdims=True)
            stat_ref[head : head + 1, rows] = peak + jnp.log2(total)
            mixed = dot_nn(vt_ref[:, pl.ds(0, keys)], weights.astype(BF16)) / total
            att_ref[rows, pl.ds(head * HD, HD)] = mixed.T.astype(BF16)


def backward_kernel(meta, q_ref, kv_ref, stat_ref, own_ref, *refs):
    received, outs, (kt_ref, g_ref, gq_ref, gk_ref, gv_ref) = refs[:3], refs[3:11], refs[11:]
    x, h = meta[0], meta[1]
    total = own_ref[...]
    for part in received:
        total = total + part[...].astype(F32)
    for head in range(HEADS):
        g_ref[head] = total[:, head * HD : (head + 1) * HD].astype(BF16)
    kt_ref[...] = kv_ref[0].astype(F32).T.astype(BF16)
    gk_ref[...] = jnp.zeros_like(gk_ref)
    gv_ref[...] = jnp.zeros_like(gv_ref)
    first = stat_ref[3:4, :].astype(jnp.int32)
    for qb in range(GROUP // QB):
        keys = (qb + 1) * QB
        rows = pl.ds(qb * QB, QB)
        span = pl.ds(0, keys)
        for head in range(HEADS):
            q = q_ref[head, rows, :]
            g = g_ref[head, rows, :]
            scores = transposed_scores(kv_ref[0, span, :], q, first[:, qb * QB : keys], qb)
            prob = jnp.exp2(scores - stat_ref[head : head + 1, rows])
            grad_prob = dot_nt(kv_ref[1, span, :], g)
            delta = jnp.sum(prob * grad_prob, axis=0, keepdims=True)
            grad_logit = (prob * (grad_prob - delta)).astype(BF16)
            gv_ref[span, :] += dot_nn(prob.astype(BF16), g)
            gk_ref[span, :] += dot_nn(grad_logit, q)
            gq = dot_nn(kt_ref[:, span], grad_logit) * SCALE
            gq_ref[head, rows, :] = gq.T.astype(BF16)
    for (dx, dh), out in zip(SHIFTS, outs):
        to_x = lax.rem(x + dx, NX)
        to_h = h if dh == 0 else 1 - h
        row = pl.multiple_of((to_x * 2 + to_h) * ROWS, ROWS)
        for head in range(HEADS):
            out[pl.ds(head * ROWS, ROWS), :] = gq_ref[head, pl.ds(row, ROWS), :]
        out[pl.ds(3 * ROWS, ROWS), :] = (gk_ref[pl.ds(row, ROWS), :] * SCALE).astype(BF16)
        out[pl.ds(4 * ROWS, ROWS), :] = gv_ref[pl.ds(row, ROWS), :].astype(BF16)


def unpack_kernel(meta, *refs):
    blocks, (gq_ref, gk_ref, gv_ref, held) = refs[:8], refs[8:]
    x, h = meta[0], meta[1]
    for (dx, dh), block in zip(SHIFTS, blocks):
        from_x = lax.rem(x - dx + NX, NX)
        from_h = h if dh == 0 else 1 - h
        source = from_h * NX + from_x
        for head in range(HEADS):
            col = pl.multiple_of(source * FEAT + head * HD, 128)
            gq_ref[:, pl.ds(col, HD)] = block[pl.ds(head * ROWS, ROWS), :]
        held[source] = block[pl.ds(3 * ROWS, 2 * ROWS), :].astype(F32)
    for head in range(4):
        both = held[2 * head] + held[2 * head + 1]
        gk_ref[:, pl.ds(head * HD, HD)] = both[:ROWS].astype(BF16)
        gv_ref[:, pl.ds(head * HD, HD)] = both[ROWS:].astype(BF16)


def weight_kernel(meta, *refs):
    mine, others, out = refs[:4], refs[4:8], refs[8]
    z, core = meta[2], meta[3]
    for dz in range(4):
        slot = lax.rem(z - dz + 4, 4)
        out[slot, pl.ds(pl.multiple_of(core * 192, 64), 192), :] = mine[dz][...]
        out[slot, pl.ds(pl.multiple_of((1 - core) * 192, 64), 192), :] = others[dz][...]


def grad_send_kernel(meta, here_ref, there_ref, w_ref, *outs):
    x = meta[0]
    for shift, out in zip((2, 1, 3), outs):
        slot = lax.rem(x + shift, NX)

        @pl.loop(0, GROUP // QB)
        def _(i):
            rows = pl.ds(pl.multiple_of(i * QB, QB), QB)
            out[rows, :] = (
                dot_nt(here_ref[rows, :], w_ref[slot, :, pl.ds(0, FEAT)])
                + dot_nt(there_ref[rows, :], w_ref[slot, :, pl.ds(FEAT, FEAT)])
            ).astype(BF16)


def grad_own_kernel(meta, here_ref, there_ref, w_ref, out):
    x = meta[0]

    @pl.loop(0, GROUP // QB)
    def _(i):
        rows = pl.ds(pl.multiple_of(i * QB, QB), QB)
        out[rows, :] = dot_nt(here_ref[rows, :], w_ref[x, :, pl.ds(0, FEAT)]) + dot_nt(
            there_ref[rows, :], w_ref[x, :, pl.ds(FEAT, FEAT)]
        )


def out_kernel(half, meta, *refs):
    att, w_ref, out = refs[:4], refs[4], refs[5]
    x = meta[0]

    @pl.loop(0, GROUP // QB)
    def _(i):
        rows = pl.ds(pl.multiple_of(i * QB, QB), QB)
        total = jnp.zeros((QB, FEAT), F32)
        for shift in range(NX):
            slot = lax.rem(x - shift + NX, NX)
            total = total + dot_nn(att[shift][rows, :], w_ref[slot, :, pl.ds(half * FEAT, FEAT)])
        out[rows, :] = total.astype(out.dtype)


def grad_weight_kernel(meta, *refs):
    att, here_ref, there_ref, keep_ref, send_ref, held = refs[:4], *refs[4:]
    x, core = meta[0], meta[3]
    for shift in range(NX):
        slot = lax.rem(x - shift + NX, NX)
        turned = att[shift][...].T
        held[:, pl.ds(0, FEAT)] = dot_nn(turned, here_ref[...])
        held[:, pl.ds(FEAT, FEAT)] = dot_nn(turned, there_ref[...])
        keep_ref[slot] = held[pl.ds(pl.multiple_of(core * 192, 64), 192), :]
        send_ref[slot] = held[pl.ds(pl.multiple_of((1 - core) * 192, 64), 192), :].astype(BF16)


def per_device(queries, key_heads, value_heads, segment_ids, out_weight, grad_out):
    dp = lax.axis_index("dp")
    cp = lax.axis_index("cp")
    x, h = cp // 2, cp % 2
    z, core = (dp // 2) % 4, dp % 2
    corner = (dp // 8) == h
    meta = jnp.stack([x, h, z, core]).astype(jnp.int32)
    both = ("dp", "cp")

    packed = call(
        pack_kernel,
        "pack",
        meta,
        (queries, key_heads, value_heads, segment_ids),
        [shaped((PACK, ROWS), BF16)] * 8,
    )
    blocks = [packed[0]] + [
        lax.ppermute(b, "cp", cp_pairs(*s)) for s, b in zip(SHIFTS[1:], packed[1:])
    ]
    grad_there = lax.ppermute(grad_out, "cp", cp_pairs(0, 1))

    swapped = lax.ppermute(out_weight, both, Y_SWAP)
    cycled = lax.ppermute(out_weight, both, Y_CYCLE_IN)
    w_here = jnp.where(corner, out_weight, cycled)
    w_there = jnp.where(corner, cycled, swapped)
    w_mine = jnp.concatenate([w_here, w_there], axis=1)
    mine = [w_mine] + [lax.ppermute(w_mine, "dp", z_pairs(dz)) for dz in (1, 2, 3)]
    others = [lax.ppermute(w, "dp", core_pairs()) for w in mine]
    (weight,) = call(
        weight_kernel, "weight", meta, (*mine, *others), [shaped((NX, FEAT, 2 * FEAT), BF16)]
    )

    attended, q_all, kv_all, stats = call(
        forward_kernel,
        "forward",
        meta,
        blocks,
        [
            shaped((GROUP, FEAT), BF16),
            shaped((HEADS, GROUP, HD), BF16),
            shaped((2, GROUP, HD), BF16),
            shaped((8, GROUP), F32),
        ],
        [pltpu.VMEM((HD, GROUP), BF16)],
        flops=2 * 2 * HEADS * GROUP * GROUP * HD,
        transcendentals=HEADS * GROUP * GROUP,
    )
    att = [attended] + [lax.ppermute(attended, "cp", cp_pairs(dx, 0)) for dx in (1, 2, 3)]

    block_flops = 2 * GROUP * FEAT * 2 * FEAT
    sends = call(
        grad_send_kernel,
        "grad_send",
        meta,
        (grad_out, grad_there, weight),
        [shaped((GROUP, FEAT), BF16)] * 3,
        flops=3 * block_flops,
    )
    parts = [lax.ppermute(p, "cp", cp_pairs(dx, 0)) for dx, p in zip((2, 1, 3), sends)]
    (own,) = call(
        grad_own_kernel,
        "grad_own",
        meta,
        (grad_out, grad_there, weight),
        [shaped((GROUP, FEAT), F32)],
        flops=block_flops,
    )

    (out_there,) = call(
        lambda *refs: out_kernel(1, *refs),
        "out_there",
        meta,
        (*att, weight),
        [shaped((GROUP, FEAT), BF16)],
        flops=2 * block_flops,
    )
    out_part = lax.ppermute(out_there, "cp", cp_pairs(0, 1))
    keep, send = call(
        grad_weight_kernel,
        "grad_weight",
        meta,
        (*att, grad_out, grad_there),
        [shaped((4, 192, 2 * FEAT), F32), shaped((4, 192, 2 * FEAT), BF16)],
        [pltpu.VMEM((FEAT, 2 * FEAT), F32)],
        flops=4 * block_flops,
    )
    core_part = lax.ppermute(send, "dp", core_pairs())
    (out_here,) = call(
        lambda *refs: out_kernel(0, *refs),
        "out_here",
        meta,
        (*att, weight),
        [shaped((GROUP, FEAT), F32)],
        flops=2 * block_flops,
    )

    def z_sum(dz):
        slot = (z + dz) % 4
        return lax.dynamic_index_in_dim(keep, slot, 0, False) + lax.dynamic_index_in_dim(
            core_part, slot, 0, False
        ).astype(F32)

    z_parts = [lax.ppermute(z_sum(dz).astype(BF16), "dp", z_pairs(dz)) for dz in (1, 2, 3)]
    z_total = z_sum(0) + sum(p.astype(F32) for p in z_parts)
    part_here, part_there = z_total[:, :FEAT], z_total[:, FEAT:]
    swap_part = lax.ppermute(part_there.astype(BF16), both, Y_SWAP)
    cycle_part = lax.ppermute(
        jnp.where(corner, part_there, part_here).astype(BF16), both, Y_CYCLE_OUT
    )
    grad_weight = jnp.where(corner, part_here, swap_part.astype(F32)) + cycle_part.astype(F32)

    output = (out_here + out_part.astype(F32)).astype(BF16)

    grads = call(
        backward_kernel,
        "backward",
        meta,
        (q_all, kv_all, stats, own, *parts),
        [shaped((5 * ROWS, ROWS), BF16)] * 8,
        [
            pltpu.VMEM((HD, GROUP), BF16),
            pltpu.VMEM((HEADS, GROUP, HD), BF16),
            pltpu.VMEM((HEADS, GROUP, HD), BF16),
            pltpu.VMEM((GROUP, HD), F32),
            pltpu.VMEM((GROUP, HD), F32),
        ],
        flops=5 * 2 * HEADS * GROUP * GROUP * HD,
        transcendentals=HEADS * GROUP * GROUP,
    )
    returned = [grads[0]] + [
        lax.ppermute(b, "cp", cp_pairs(*s)) for s, b in zip(SHIFTS[1:], grads[1:])
    ]
    grad_queries, grad_keys, grad_values = call(
        unpack_kernel,
        "unpack",
        meta,
        returned,
        [shaped((ROWS, 8 * FEAT), BF16), shaped((ROWS, 4 * HD), BF16), shaped((ROWS, 4 * HD), BF16)],
        [pltpu.VMEM((8, 2 * ROWS, HD), F32)],
    )
    return output, grad_queries, grad_keys, grad_values, grad_weight


def solution(mesh):
    in_specs = (
        P(("dp", "cp"), None),
        P(("dp", "cp"), None),
        P(("dp", "cp"), None),
        P("dp", "cp"),
        P("dp", "cp"),
        P("dp", "cp"),
    )
    out_specs = (
        P("dp", "cp"),
        P(("dp", "cp"), None),
        P(("dp", "cp"), None),
        P(("dp", "cp"), None),
        P("dp", "cp"),
    )
    return jax.shard_map(
        per_device, mesh=mesh, in_specs=in_specs, out_specs=out_specs, check_vma=False
    )
```

```python
import math

import jax
import jax.numpy as jnp
from jax import lax
from jax.experimental import pallas as pl
from jax.experimental.pallas import tpu as pltpu
from jax.sharding import PartitionSpec as P


NX = 4
GROUP = 1024
HD = 128
HEADS = 3
FEAT = 384
ROWS = 128
QB = 256
SEG_ROWS = 16
PACK = 5 * ROWS + SEG_ROWS
SCALE = 1.0 / math.sqrt(HD)
EXP2_SCALE = SCALE * math.log2(math.e)
F32 = jnp.float32
BF16 = jnp.bfloat16


def cp_pairs(dx, dh):
    return [(x * 2 + h, ((x + dx) % NX) * 2 + (h ^ dh)) for x in range(NX) for h in range(2)]


def z_pairs(dz):
    return [
        (y * 8 + z * 2 + c, y * 8 + ((z + dz) % 4) * 2 + c)
        for y in range(2)
        for z in range(4)
        for c in range(2)
    ]


def core_pairs():
    return [(d, d ^ 1) for d in range(16)]


def x_to_z_pairs(dy):
    return [
        (((y * 4 + z) * 2 + c) * 8 + x * 2 + h, (((y ^ dy) * 4 + x) * 2 + c) * 8 + z * 2 + h)
        for y in range(2)
        for z in range(4)
        for c in range(2)
        for x in range(4)
        for h in range(2)
    ]


def dot_nt(a, b):
    return lax.dot_general(a, b, (((1,), (1,)), ((), ())), preferred_element_type=F32)


def dot_nn(a, b):
    return lax.dot_general(a, b, (((1,), (0,)), ((), ())), preferred_element_type=F32)


def dot_tn(a, b):
    return lax.dot_general(a, b, (((0,), (0,)), ((), ())), preferred_element_type=F32)


def call(kernel, name, meta, operands, outs, scratch=(), span=0, after=(), hbm=(), vmem=48):
    count = len(operands)

    def body(meta_ref, *refs):
        kernel(meta_ref, *refs[:count], *refs[count + len(after) :])

    return pl.pallas_call(
        body,
        name=name,
        out_shape=tuple(outs),
        in_specs=[pl.BlockSpec(memory_space=pltpu.SMEM)]
        + [pl.BlockSpec(memory_space=pl.ANY if i in hbm else pltpu.VMEM) for i in range(count)]
        + [pl.BlockSpec(memory_space=pl.ANY)] * len(after),
        out_specs=tuple(pl.BlockSpec(memory_space=pltpu.VMEM) for _ in outs),
        scratch_shapes=list(scratch),
        compiler_params=pltpu.CompilerParams(vmem_limit_bytes=vmem * 1024 * 1024),
        cost_estimate=pl.CostEstimate(flops=span * 10**9, bytes_accessed=0, transcendentals=0),
    )(meta, *operands, *after)


def shaped(shape, dtype):
    return jax.ShapeDtypeStruct(shape, dtype)


def pack_kernel(meta, q_ref, k_ref, v_ref, seg_ref, out, sems):
    copies = []
    for to in range(8):
        to_x, to_h = to // 2, to % 2
        q_off = (to_h * NX + to_x) * FEAT
        kv_off = (to_h * 2 + to_x // 2) * HD
        sources = [q_ref.at[:, pl.ds(q_off + head * HD, HD)] for head in range(HEADS)]
        sources += [k_ref.at[:, pl.ds(kv_off, HD)], v_ref.at[:, pl.ds(kv_off, HD)]]
        for i, source in enumerate(sources):
            copies.append(
                pltpu.make_async_copy(source, out.at[to, pl.ds(i * ROWS, ROWS), :], sems.at[to, i])
            )
            copies[-1].start()
    seg = jnp.broadcast_to(seg_ref[...].astype(F32), (SEG_ROWS, ROWS)).astype(BF16)
    for to in range(8):
        out[to, pl.ds(5 * ROWS, SEG_ROWS), :] = seg
    for copy in copies:
        copy.wait()


def transposed_scores(k, q, first, qb):
    scores = dot_nt(k, q)
    key_pos = lax.broadcasted_iota(jnp.int32, scores.shape, 0)
    query_pos = lax.broadcasted_iota(jnp.int32, scores.shape, 1) + qb * QB
    return jnp.where((key_pos <= query_pos) & (key_pos >= first), scores * EXP2_SCALE, -1e30)


def forward_kernel(meta, *refs):
    blocks, (att_ref, q_ref, kv_ref, stat_ref, vt_ref) = refs[0], refs[1:]
    seg_sum = jnp.zeros((1, ROWS), F32)
    for source in range(8):
        rows = pl.ds(source * ROWS, ROWS)
        for head in range(HEADS):
            q_ref[head, rows, :] = blocks[source, pl.ds(head * ROWS, ROWS), :]
        kv_ref[0, rows, :] = blocks[source, pl.ds(3 * ROWS, ROWS), :]
        kv_ref[1, rows, :] = blocks[source, pl.ds(4 * ROWS, ROWS), :]
        seg_sum = seg_sum + blocks[source, pl.ds(5 * ROWS, SEG_ROWS), :].astype(F32)[0:1]
    second = jnp.sum(seg_sum, axis=1, keepdims=True)
    boundary = (GROUP - second).astype(jnp.int32)
    position = lax.broadcasted_iota(jnp.int32, (1, GROUP), 1)
    first = jnp.where(position >= boundary, boundary, 0)
    stat_ref[...] = jnp.zeros_like(stat_ref)
    stat_ref[3:4, :] = first.astype(F32)
    vt_ref[...] = kv_ref[1].astype(F32).T.astype(BF16)
    for qb in range(GROUP // QB):
        keys = (qb + 1) * QB
        rows = pl.ds(qb * QB, QB)
        for head in range(HEADS):
            scores = transposed_scores(
                kv_ref[0, pl.ds(0, keys), :], q_ref[head, rows, :], first[:, qb * QB : keys], qb
            )
            peak = jnp.max(scores, axis=0, keepdims=True)
            weights = jnp.exp2(scores - peak)
            total = jnp.sum(weights, axis=0, keepdims=True)
            stat_ref[head : head + 1, rows] = peak + jnp.log2(total)
            mixed = dot_nn(vt_ref[:, pl.ds(0, keys)], weights.astype(BF16)) / total
            att_ref[rows, pl.ds(head * HD, HD)] = mixed.T.astype(BF16)


def backward_kernel(meta, q_ref, kv_ref, stat_ref, own_ref, *refs):
    high_ref, low_ref, out, kt_ref, g_ref, gq_ref, gk_ref, gv_ref = refs
    half = GROUP // 2
    for received, first in ((low_ref, 0), (high_ref, half)):
        total = own_ref[pl.ds(first, half), :] + received[...].astype(F32)
        for head in range(HEADS):
            g_ref[head, pl.ds(first, half), :] = total[:, head * HD : (head + 1) * HD].astype(BF16)
    kt_ref[...] = kv_ref[0].astype(F32).T.astype(BF16)
    gk_ref[...] = jnp.zeros_like(gk_ref)
    gv_ref[...] = jnp.zeros_like(gv_ref)
    first = stat_ref[3:4, :].astype(jnp.int32)
    for qb in range(GROUP // QB):
        keys = (qb + 1) * QB
        rows = pl.ds(qb * QB, QB)
        span = pl.ds(0, keys)
        for head in range(HEADS):
            q = q_ref[head, rows, :]
            g = g_ref[head, rows, :]
            scores = transposed_scores(kv_ref[0, span, :], q, first[:, qb * QB : keys], qb)
            prob = jnp.exp2(scores - stat_ref[head : head + 1, rows])
            grad_prob = dot_nt(kv_ref[1, span, :], g)
            delta = jnp.sum(prob * grad_prob, axis=0, keepdims=True)
            grad_logit = (prob * (grad_prob - delta)).astype(BF16)
            gv_ref[span, :] += dot_nn(prob.astype(BF16), g)
            gk_ref[span, :] += dot_nn(grad_logit, q)
            gq = dot_nn(kt_ref[:, span], grad_logit) * SCALE
            gq_ref[head, rows, :] = gq.T.astype(BF16)
    for to in range(8):
        rows = pl.ds(to * ROWS, ROWS)
        for head in range(HEADS):
            out[to, pl.ds(head * ROWS, ROWS), :] = gq_ref[head, rows, :]
        out[to, pl.ds(3 * ROWS, ROWS), :] = (gk_ref[rows, :] * SCALE).astype(BF16)
        out[to, pl.ds(4 * ROWS, ROWS), :] = gv_ref[rows, :].astype(BF16)


def unpack_kernel(meta, blocks, gq_ref, gk_ref, gv_ref):
    def block(head, first):
        return blocks[(head % NX) * 2 + head // NX, pl.ds(first * ROWS, ROWS), :]

    for source in range(8):
        for head in range(HEADS):
            gq_ref[:, pl.ds(source * FEAT + head * HD, HD)] = block(source, head)
    for head in range(4):
        cols = pl.ds(head * HD, HD)
        for first, out in ((3, gk_ref), (4, gv_ref)):
            both = block(2 * head, first).astype(F32) + block(2 * head + 1, first).astype(F32)
            out[:, cols] = both.astype(BF16)


def gather_columns(x, refs, out):
    own, right, left, low, high = refs
    half = GROUP // 2
    out[:, pl.ds(0, FEAT)] = own[...]
    out[:, pl.ds(FEAT, FEAT)] = right[...]
    out[pl.ds(0, half), pl.ds(2 * FEAT, FEAT)] = low[...]
    out[pl.ds(half, half), pl.ds(2 * FEAT, FEAT)] = high[...]
    out[:, pl.ds(3 * FEAT, FEAT)] = left[...]


def place_weight(meta, w_ref, part, column, out, row, col):
    which = jnp.where(part == meta[4], 0, 1)
    for core in range(2):
        out[pl.ds(row + core * 192, 192), pl.ds(col, FEAT)] = w_ref[column, core, which]


def grad_kernel(meta, *refs):
    grads, w_ref, high_ref, low_ref, own_ref, held, wide = refs[:5], *refs[5:]
    x, h = meta[0], meta[1]
    gather_columns(x, grads, held)
    for shift in range(NX):
        slot = lax.rem(x - shift + NX, NX)
        place_weight(meta, w_ref, 1 - h, slot, wide, 0, shift * FEAT)
        place_weight(meta, w_ref, h, slot, wide, FEAT, shift * FEAT)

    for send, first in ((high_ref, GROUP // 2), (low_ref, 0)):

        @pl.loop(0, GROUP // QB // 2)
        def _(i):
            row = pl.multiple_of(i * QB, QB)
            rows = pl.ds(row + first, QB)
            total = dot_nt(held[rows, :], wide[...])
            send[pl.ds(row, QB), :] = total[:, :FEAT].astype(BF16)
            own_ref[rows, :] = total[:, FEAT:]


def out_kernel(meta, here_ref, there_ref, w_ref, out, wide):
    h = meta[1]
    for column in range(NX):
        place_weight(meta, w_ref, h, column, wide, 0, column * FEAT)
        place_weight(meta, w_ref, 1 - h, column, wide, FEAT, column * FEAT)

    @pl.loop(0, GROUP // QB)
    def _(i):
        rows = pl.ds(pl.multiple_of(i * QB, QB), QB)
        total = dot_nn(here_ref[rows, :], wide[pl.ds(0, FEAT), :]) + dot_nn(
            there_ref[rows, :], wide[pl.ds(FEAT, FEAT), :]
        )
        for column in range(NX):
            out[column, rows, :] = total[:, column * FEAT : (column + 1) * FEAT].astype(BF16)


def grad_weight_kernel(meta, *refs):
    att, grads, (keep_ref, *sends, held, total) = refs[:2], refs[2:7], refs[7:]
    x, h, core = meta[0], meta[1], meta[3]
    gather_columns(x, grads, held)
    for which in range(2):
        part = h if which == 0 else 1 - h
        turned = att[which][...].T
        total[...] = dot_nn(turned, held[...])
        for shift in range(NX):
            slot = lax.rem(x - shift + NX, NX)
            cols = pl.ds(shift * FEAT, FEAT)
            keep_ref[part, slot] = total[pl.ds(pl.multiple_of(core * 192, 64), 192), cols]
            for part_rows in range(2):
                row = pl.multiple_of((1 - core) * 192 + part_rows * 96, 32)
                sends[which * 2 + part_rows][slot] = total[pl.ds(row, 96), cols].astype(BF16)


def z_kernel(meta, keep_ref, *refs):
    parts, own_ref, outs = refs[:4], refs[4], refs[5:]
    h, z = meta[1], meta[2]
    for dz in range(4):
        slot = lax.rem(z + dz, 4)
        for which, row in ((0, h), (1, 1 - h)):
            for part_rows in range(2):
                rows = pl.ds(part_rows * 96, 96)
                total = keep_ref[row, slot, rows, :] + parts[which * 2 + part_rows][slot].astype(F32)
                if dz == 0:
                    own_ref[row, rows, :] = total
                else:
                    outs[dz - 1][row, rows, :] = total.astype(BF16)


def y_kernel(meta, own_ref, *refs):
    parts, (keep_ref, send_ref) = refs[:3], refs[3:]
    y_lo = meta[4]
    for which, out in ((y_lo, keep_ref), (1 - y_lo, send_ref)):
        total = own_ref[which]
        for part in parts:
            total = total + part[which].astype(F32)
        out[...] = total.astype(out.dtype)


def sum_kernel(meta, a_ref, b_ref, out):
    out[...] = a_ref[...].astype(F32) + b_ref[...].astype(F32)


def stack_kernel(meta, a_ref, b_ref, grad_ref, out, grad_out, sem):
    copy = pltpu.make_async_copy(grad_ref, grad_out, sem)
    copy.start()
    out[0] = a_ref[...]
    out[1] = b_ref[...]
    copy.wait()


def per_device(queries, key_heads, value_heads, segment_ids, out_weight, grad_out):
    dp = lax.axis_index("dp")
    cp = lax.axis_index("cp")
    x, h = cp // 2, cp % 2
    y_lo, z, core = dp // 8, (dp // 2) % 4, dp % 2
    meta = jnp.stack([x, h, z, core, y_lo]).astype(jnp.int32)
    both = ("dp", "cp")
    half = GROUP // 2

    turned = [lax.ppermute(out_weight, both, x_to_z_pairs(dy)) for dy in (0, 1)]
    (packed,) = call(
        pack_kernel,
        "pack",
        meta,
        (queries, key_heads, value_heads, segment_ids),
        [shaped((8, PACK, ROWS), BF16)],
        [pltpu.SemaphoreType.DMA((8, 5))],
        hbm=(0, 1, 2),
        vmem=60,
    )
    blocks = lax.all_to_all(packed, "cp", 0, 0)
    turned, grad_out = call(
        stack_kernel,
        "turned",
        meta,
        (*turned, grad_out),
        [shaped((2, 192, FEAT), BF16), shaped((GROUP, FEAT), BF16)],
        [pltpu.SemaphoreType.DMA],
        span=20,
        after=(packed,),
        hbm=(2,),
    )
    from_left = lax.ppermute(grad_out, "cp", cp_pairs(1, 0))
    from_right = lax.ppermute(grad_out, "cp", cp_pairs(3, 0))
    weight = lax.all_gather(
        turned, "dp", axis=0, axis_index_groups=[list(range(8)), list(range(8, 16))]
    ).reshape(NX, 2, 2, 192, FEAT)
    low = lax.ppermute(from_left[:half], "cp", cp_pairs(1, 0))
    high = lax.ppermute(from_right[half:], "cp", cp_pairs(3, 0))
    grads_out = (grad_out, from_left, from_right, low, high)

    attended, q_all, kv_all, stats = call(
        forward_kernel,
        "forward",
        meta,
        (blocks,),
        [
            shaped((GROUP, FEAT), BF16),
            shaped((HEADS, GROUP, HD), BF16),
            shaped((2, GROUP, HD), BF16),
            shaped((8, GROUP), F32),
        ],
        [pltpu.VMEM((HD, GROUP), BF16)],
        span=100,
    )
    att = (attended, lax.ppermute(attended, "cp", cp_pairs(0, 1)))

    send_high, send_low, grad_own = call(
        grad_kernel,
        "grad_attended",
        meta,
        (*grads_out, weight),
        [shaped((half, FEAT), BF16)] * 2 + [shaped((GROUP, FEAT), F32)],
        [pltpu.VMEM((GROUP, NX * FEAT), BF16), pltpu.VMEM((2 * FEAT, NX * FEAT), BF16)],
        after=(attended,),
    )
    part_high = lax.ppermute(send_high, "cp", cp_pairs(0, 1))
    part_low = lax.ppermute(send_low, "cp", cp_pairs(0, 1))

    (out_all,) = call(
        out_kernel,
        "out",
        meta,
        (*att, weight),
        [shaped((NX, GROUP, FEAT), BF16)],
        [pltpu.VMEM((2 * FEAT, NX * FEAT), BF16)],
        after=(grad_own,),
        span=20,
    )
    output = lax.psum_scatter(
        out_all,
        "cp",
        scatter_dimension=0,
        axis_index_groups=[[x * 2 + h for x in range(NX)] for h in range(2)],
    )

    keep, *sends = call(
        grad_weight_kernel,
        "grad_weight",
        meta,
        (*att, *grads_out),
        [shaped((2, NX, 192, FEAT), F32)] + [shaped((NX, 96, FEAT), BF16)] * 4,
        [pltpu.VMEM((GROUP, NX * FEAT), BF16), pltpu.VMEM((FEAT, NX * FEAT), F32)],
        after=(out_all, part_high),
        span=80,
    )
    core_parts = [lax.ppermute(p, "dp", core_pairs()) for p in sends]

    z_own, *z_sends = call(
        z_kernel,
        "z_sum",
        meta,
        (keep, *core_parts),
        [shaped((2, 192, FEAT), F32)] + [shaped((2, 192, FEAT), BF16)] * 3,
        after=(part_low,),
    )
    z_parts = [lax.ppermute(p, "dp", z_pairs(dz)) for dz, p in zip((1, 2, 3), z_sends)]

    (grads,) = call(
        backward_kernel,
        "backward",
        meta,
        (q_all, kv_all, stats, grad_own, part_high, part_low),
        [shaped((8, 5 * ROWS, ROWS), BF16)],
        [
            pltpu.VMEM((HD, GROUP), BF16),
            pltpu.VMEM((HEADS, GROUP, HD), BF16),
            pltpu.VMEM((HEADS, GROUP, HD), BF16),
            pltpu.VMEM((GROUP, HD), F32),
            pltpu.VMEM((GROUP, HD), F32),
        ],
        after=(z_own,),
    )
    returned = lax.all_to_all(grads, "cp", 0, 0)

    y_own, y_send = call(
        y_kernel,
        "y_sum",
        meta,
        (z_own, *z_parts),
        [shaped((192, FEAT), BF16), shaped((192, FEAT), BF16)],
        after=(grads,),
        span=15,
    )
    totals = [lax.ppermute(p, both, x_to_z_pairs(dy)) for dy, p in ((0, y_own), (1, y_send))]
    (grad_weight,) = call(sum_kernel, "grad_weight_total", meta, totals, [shaped((192, FEAT), F32)])

    grad_queries, grad_keys, grad_values = call(
        unpack_kernel,
        "unpack",
        meta,
        (returned,),
        [shaped((ROWS, 8 * FEAT), BF16), shaped((ROWS, 4 * HD), BF16), shaped((ROWS, 4 * HD), BF16)],
    )
    return output, grad_queries, grad_keys, grad_values, grad_weight


def solution(mesh):
    in_specs = (
        P(("dp", "cp"), None),
        P(("dp", "cp"), None),
        P(("dp", "cp"), None),
        P("dp", "cp"),
        P("dp", "cp"),
        P("dp", "cp"),
    )
    out_specs = (
        P("dp", "cp"),
        P(("dp", "cp"), None),
        P(("dp", "cp"), None),
        P(("dp", "cp"), None),
        P("dp", "cp"),
    )
    return jax.shard_map(
        per_device, mesh=mesh, in_specs=in_specs, out_specs=out_specs, check_vma=False
    )
```

```python
import math

import jax
import jax.numpy as jnp
from jax import lax
from jax.experimental import pallas as pl
from jax.experimental.pallas import tpu as pltpu
from jax.sharding import PartitionSpec as P


NX = 4
GROUP = 1024
HD = 128
HEADS = 3
FEAT = 384
ROWS = 128
QB = 256
SEG_ROWS = 16
PACK = 5 * ROWS + SEG_ROWS
SCALE = 1.0 / math.sqrt(HD)
FAR = -(2.0**17)
EXP2_SCALE = SCALE * math.log2(math.e)
F32 = jnp.float32
BF16 = jnp.bfloat16


def cp_pairs(dx, dh):
    return [(x * 2 + h, ((x + dx) % NX) * 2 + (h ^ dh)) for x in range(NX) for h in range(2)]


def z_pairs(dz):
    return [
        (y * 8 + z * 2 + c, y * 8 + ((z + dz) % 4) * 2 + c)
        for y in range(2)
        for z in range(4)
        for c in range(2)
    ]


def core_pairs():
    return [(d, d ^ 1) for d in range(16)]


def x_to_z_pairs(dy):
    return [
        (((y * 4 + z) * 2 + c) * 8 + x * 2 + h, (((y ^ dy) * 4 + x) * 2 + c) * 8 + z * 2 + h)
        for y in range(2)
        for z in range(4)
        for c in range(2)
        for x in range(4)
        for h in range(2)
    ]


def dot_nt(a, b):
    return lax.dot_general(a, b, (((1,), (1,)), ((), ())), preferred_element_type=F32)


def dot_nn(a, b):
    return lax.dot_general(a, b, (((1,), (0,)), ((), ())), preferred_element_type=F32)


def dot_tn(a, b):
    return lax.dot_general(a, b, (((0,), (0,)), ((), ())), preferred_element_type=F32)


def call(
    kernel, name, meta, operands, outs, scratch=(), span=0, after=(), hbm=(), vmem=32, grid=(), blocks=None, out_blocks=None
):
    count = len(operands)

    def body(meta_ref, *refs):
        kernel(meta_ref, *refs[:count], *refs[count + len(after) :])

    def whole(i):
        return pl.BlockSpec(memory_space=pl.ANY if i in hbm else pltpu.VMEM)

    return pl.pallas_call(
        body,
        name=name,
        out_shape=tuple(outs),
        grid=grid,
        in_specs=[pl.BlockSpec(memory_space=pltpu.SMEM)]
        + (blocks or [whole(i) for i in range(count)])
        + [pl.BlockSpec(memory_space=pl.ANY)] * len(after),
        out_specs=tuple(out_blocks or [pl.BlockSpec(memory_space=pltpu.VMEM) for _ in outs]),
        scratch_shapes=list(scratch),
        compiler_params=pltpu.CompilerParams(vmem_limit_bytes=vmem * 1024 * 1024),
        cost_estimate=pl.CostEstimate(flops=span * 10**9, bytes_accessed=0, transcendentals=0),
    )(meta, *operands, *after)


def row_block(height, width, index):
    return pl.BlockSpec((height, width), lambda i: (index(i), 0))


def whole_block(shape):
    return pl.BlockSpec(shape, lambda i: (0,) * len(shape))


def shaped(shape, dtype):
    return jax.ShapeDtypeStruct(shape, dtype)


def pack_kernel(meta, q_ref, k_ref, v_ref, seg_ref, out, sems):
    copies = []
    for to in range(8):
        to_x, to_h = to // 2, to % 2
        q_off = (to_h * NX + to_x) * FEAT
        kv_off = (to_h * 2 + to_x // 2) * HD
        sources = [q_ref.at[:, pl.ds(q_off + head * HD, HD)] for head in range(HEADS)]
        sources += [k_ref.at[:, pl.ds(kv_off, HD)], v_ref.at[:, pl.ds(kv_off, HD)]]
        for i, source in enumerate(sources):
            copies.append(
                pltpu.make_async_copy(source, out.at[to, pl.ds(i * ROWS, ROWS), :], sems.at[to, i])
            )
            copies[-1].start()
    seg = jnp.broadcast_to(seg_ref[...].astype(F32), (SEG_ROWS, ROWS)).astype(BF16)
    for to in range(8):
        out[to, pl.ds(5 * ROWS, SEG_ROWS), :] = seg
    for copy in copies:
        copy.wait()


def key_parts(qb):
    start = QB if qb == 3 else 0
    return [r for r in ((start, qb * QB, False), (qb * QB, (qb + 1) * QB, True)) if r[0] < r[1]]


def widen(boundary, q_ref, k_ref, q_wide, k_wide):
    shape = (GROUP, HD)
    column = lax.broadcasted_iota(jnp.int32, shape, 1) == 0
    second = lax.broadcasted_iota(jnp.int32, shape, 0) >= boundary
    q_more = jnp.where(column & second, FAR, 0.0).astype(BF16)
    k_more = jnp.where(column & jnp.logical_not(second), 1.0, 0.0).astype(BF16)
    for head in range(HEADS):
        q_wide[head, :, pl.ds(0, HD)] = q_ref[head]
        q_wide[head, :, pl.ds(HD, HD)] = q_more
    k_wide[:, pl.ds(0, HD)] = k_ref[0]
    k_wide[:, pl.ds(HD, HD)] = k_more


def transposed_scores(k, q, diagonal):
    scores = dot_nt(k, q) * EXP2_SCALE
    if diagonal:
        key_pos = lax.broadcasted_iota(jnp.int32, scores.shape, 0)
        query_pos = lax.broadcasted_iota(jnp.int32, scores.shape, 1)
        scores = jnp.where(key_pos <= query_pos, scores, -1e30)
    return scores


def forward_rows(qbs, q_wide, k_wide, vt_ref, att_ref, stat_ref):
    base = qbs[0] * QB
    for qb in qbs:
        out_rows = pl.ds(qb * QB - base, QB)
        for head in range(HEADS):
            q = q_wide[head, pl.ds(qb * QB, QB), :]
            parts = [
                (pl.ds(lo, hi - lo), transposed_scores(k_wide[pl.ds(lo, hi - lo), :], q, diagonal))
                for lo, hi, diagonal in key_parts(qb)
            ]
            peaks = [jnp.max(scores, axis=0, keepdims=True) for _, scores in parts]
            peak = peaks[0] if len(peaks) == 1 else jnp.maximum(*peaks)
            total, mixed = 0.0, 0.0
            for span, scores in parts:
                weights = jnp.exp2(scores - peak)
                total = total + jnp.sum(weights, axis=0, keepdims=True)
                mixed = mixed + dot_nn(vt_ref[:, span], weights.astype(BF16))
            stat_ref[head : head + 1, out_rows] = peak + jnp.log2(total)
            att_ref[out_rows, pl.ds(head * HD, HD)] = (mixed / total).T.astype(BF16)


def forward_low_kernel(
    meta, blocks, att_ref, q_ref, kv_ref, vt_ref, boundary_ref, stat_ref, q_wide, k_wide
):
    seg_sum = jnp.zeros((1, ROWS), F32)
    for source in range(8):
        rows = pl.ds(source * ROWS, ROWS)
        for head in range(HEADS):
            q_ref[head, rows, :] = blocks[source, pl.ds(head * ROWS, ROWS), :]
        kv_ref[0, rows, :] = blocks[source, pl.ds(3 * ROWS, ROWS), :]
        kv_ref[1, rows, :] = blocks[source, pl.ds(4 * ROWS, ROWS), :]
        seg_sum = seg_sum + blocks[source, pl.ds(5 * ROWS, SEG_ROWS), :].astype(F32)[0:1]
    second = jnp.sum(seg_sum, axis=1, keepdims=True)
    boundary = (GROUP - second).astype(jnp.int32)
    boundary_ref[...] = jnp.broadcast_to(boundary, boundary_ref.shape)
    vt_ref[...] = kv_ref[1].astype(F32).T.astype(BF16)
    stat_ref[...] = jnp.zeros_like(stat_ref)
    widen(boundary, q_ref, kv_ref, q_wide, k_wide)
    forward_rows((0, 1), q_wide, k_wide, vt_ref, att_ref, stat_ref)


def forward_high_kernel(meta, q_ref, kv_ref, vt_ref, boundary_ref, att_ref, stat_ref, q_wide, k_wide):
    stat_ref[...] = jnp.zeros_like(stat_ref)
    widen(boundary_ref[0:1, 0:1], q_ref, kv_ref, q_wide, k_wide)
    forward_rows((2, 3), q_wide, k_wide, vt_ref, att_ref, stat_ref)


def backward_kernel(meta, q_ref, kv_ref, boundary_ref, stat_low, stat_high, own_ref, *refs):
    part_ref, out, kt_ref, g_ref, gq_ref, gk_ref, gv_ref, q_wide, k_wide = refs
    total = own_ref[...] + part_ref[...].astype(F32)
    for head in range(HEADS):
        g_ref[head] = total[:, head * HD : (head + 1) * HD].astype(BF16)
    kt_ref[...] = kv_ref[0].astype(F32).T.astype(BF16)
    gk_ref[...] = jnp.zeros_like(gk_ref)
    gv_ref[...] = jnp.zeros_like(gv_ref)
    widen(boundary_ref[0:1, 0:1], q_ref, kv_ref, q_wide, k_wide)
    for qb in range(GROUP // QB):
        rows = pl.ds(qb * QB, QB)
        stat_ref, stat_rows = (stat_low, rows) if qb < 2 else (stat_high, pl.ds(qb * QB - GROUP // 2, QB))
        for head in range(HEADS):
            q = q_ref[head, rows, :]
            g = g_ref[head, rows, :]
            parts, delta = [], 0.0
            for lo, hi, diagonal in key_parts(qb):
                span = pl.ds(lo, hi - lo)
                scores = transposed_scores(k_wide[span, :], q_wide[head, rows, :], diagonal)
                prob = jnp.exp2(scores - stat_ref[head : head + 1, stat_rows])
                grad_prob = dot_nt(kv_ref[1, span, :], g)
                delta = delta + jnp.sum(prob * grad_prob, axis=0, keepdims=True)
                gv_ref[span, :] += dot_nn(prob.astype(BF16), g)
                parts.append((span, prob, grad_prob))
            gq = 0.0
            for span, prob, grad_prob in parts:
                grad_logit = (prob * (grad_prob - delta)).astype(BF16)
                gk_ref[span, :] += dot_nn(grad_logit, q)
                gq = gq + dot_nn(kt_ref[:, span], grad_logit)
            gq_ref[head, rows, :] = (gq * SCALE).T.astype(BF16)
    for to in range(8):
        rows = pl.ds(to * ROWS, ROWS)
        for head in range(HEADS):
            out[to, pl.ds(head * ROWS, ROWS), :] = gq_ref[head, rows, :]
        out[to, pl.ds(3 * ROWS, ROWS), :] = (gk_ref[rows, :] * SCALE).astype(BF16)
        out[to, pl.ds(4 * ROWS, ROWS), :] = gv_ref[rows, :].astype(BF16)


def unpack_kernel(meta, blocks, gq_ref, gk_ref, gv_ref):
    def block(head, first):
        return blocks[(head % NX) * 2 + head // NX, pl.ds(first * ROWS, ROWS), :]

    for source in range(8):
        for head in range(HEADS):
            gq_ref[:, pl.ds(source * FEAT + head * HD, HD)] = block(source, head)
    for head in range(4):
        cols = pl.ds(head * HD, HD)
        for first, out in ((3, gk_ref), (4, gv_ref)):
            both = block(2 * head, first).astype(F32) + block(2 * head + 1, first).astype(F32)
            out[:, cols] = both.astype(BF16)


def gather_columns(x, refs, out):
    own, right, left, low, high = refs
    half = GROUP // 2
    out[:, pl.ds(0, FEAT)] = own[...]
    out[:, pl.ds(FEAT, FEAT)] = right[...]
    out[pl.ds(0, half), pl.ds(2 * FEAT, FEAT)] = low[...]
    out[pl.ds(half, half), pl.ds(2 * FEAT, FEAT)] = high[...]
    out[:, pl.ds(3 * FEAT, FEAT)] = left[...]


def place_weight(meta, w_ref, part, column, out, row, col):
    which = jnp.where(part == meta[4], 0, 1)
    for core in range(2):
        out[pl.ds(row + core * 192, 192), pl.ds(col, FEAT)] = w_ref[column, core, which]


def grad_kernel(meta, *refs):
    grads, w_ref, send_ref, own_ref, held, wide = refs[:5], *refs[5:]
    x, h = meta[0], meta[1]
    step = pl.program_id(0)

    @pl.when(step == 0)
    def _():
        for shift in range(NX):
            slot = lax.rem(x - shift + NX, NX)
            place_weight(meta, w_ref, 1 - h, slot, wide, 0, shift * FEAT)
            place_weight(meta, w_ref, h, slot, wide, FEAT, shift * FEAT)

    own, right, left, low, high = grads
    for shift, part in ((0, own), (1, right), (3, left)):
        held[:, pl.ds(shift * FEAT, FEAT)] = part[...]
    far = pl.ds(2 * FEAT, FEAT)
    is_high = step >= 2

    @pl.when(is_high)
    def _():
        held[:, far] = high[...]

    @pl.when(jnp.logical_not(is_high))
    def _():
        held[:, far] = low[...]

    total = dot_nt(held[...], wide[...])
    send_ref[...] = total[:, :FEAT].astype(BF16)
    own_ref[...] = total[:, FEAT:]


def out_kernel(meta, here_low, here_high, there_low, there_high, w_ref, out, wide):
    h = meta[1]
    is_low = pl.program_id(0) < 2

    @pl.when(pl.program_id(0) == 0)
    def _():
        for column in range(NX):
            place_weight(meta, w_ref, h, column, wide, 0, column * FEAT)
            place_weight(meta, w_ref, 1 - h, column, wide, FEAT, column * FEAT)

    here = jnp.where(is_low, here_low[...], here_high[...])
    there = jnp.where(is_low, there_low[...], there_high[...])
    total = dot_nn(here, wide[pl.ds(0, FEAT), :]) + dot_nn(there, wide[pl.ds(FEAT, FEAT), :])
    for column in range(NX):
        out[column] = total[:, column * FEAT : (column + 1) * FEAT].astype(BF16)


def grad_weight_kernel(meta, *refs):
    att, grads, (keep_ref, *sends, held, total) = refs[:4], refs[4:9], refs[9:]
    half = GROUP // 2
    x, h, core = meta[0], meta[1], meta[3]
    gather_columns(x, grads, held)
    for which in range(2):
        part = h if which == 0 else 1 - h
        low, high = att[2 * which][...].T, att[2 * which + 1][...].T
        total[...] = dot_nn(low, held[pl.ds(0, half), :]) + dot_nn(high, held[pl.ds(half, half), :])
        for shift in range(NX):
            slot = lax.rem(x - shift + NX, NX)
            cols = pl.ds(shift * FEAT, FEAT)
            keep_ref[part, slot] = total[pl.ds(pl.multiple_of(core * 192, 64), 192), cols]
            for part_rows in range(2):
                row = pl.multiple_of((1 - core) * 192 + part_rows * 96, 32)
                sends[which * 2 + part_rows][slot] = total[pl.ds(row, 96), cols].astype(BF16)


def z_kernel(meta, keep_ref, *refs):
    parts, own_ref, outs = refs[:4], refs[4], refs[5:]
    h, z = meta[1], meta[2]
    for dz in range(4):
        slot = lax.rem(z + dz, 4)
        for which, row in ((0, h), (1, 1 - h)):
            for part_rows in range(2):
                rows = pl.ds(part_rows * 96, 96)
                total = keep_ref[row, slot, rows, :] + parts[which * 2 + part_rows][slot].astype(F32)
                if dz == 0:
                    own_ref[row, rows, :] = total
                else:
                    outs[dz - 1][row, rows, :] = total.astype(BF16)


def y_kernel(meta, own_ref, *refs):
    parts, (keep_ref, send_ref) = refs[:3], refs[3:]
    y_lo = meta[4]
    for which, out in ((y_lo, keep_ref), (1 - y_lo, send_ref)):
        total = own_ref[which]
        for part in parts:
            total = total + part[which].astype(F32)
        out[...] = total.astype(out.dtype)


def sum_kernel(meta, a_ref, b_ref, out):
    out[...] = a_ref[...].astype(F32) + b_ref[...].astype(F32)


def stack_kernel(meta, a_ref, b_ref, grad_ref, out, grad_out, sem):
    copy = pltpu.make_async_copy(grad_ref, grad_out, sem)
    copy.start()
    out[0] = a_ref[...]
    out[1] = b_ref[...]
    copy.wait()


def halves_kernel(meta, left_ref, right_ref, low_ref, high_ref, sems):
    half = low_ref.shape[0]
    copies = [
        pltpu.make_async_copy(left_ref.at[pl.ds(0, half), :], low_ref, sems.at[0]),
        pltpu.make_async_copy(right_ref.at[pl.ds(half, half), :], high_ref, sems.at[1]),
    ]
    for copy in copies:
        copy.start()
    for copy in copies:
        copy.wait()


def per_device(queries, key_heads, value_heads, segment_ids, out_weight, grad_out):
    dp = lax.axis_index("dp")
    cp = lax.axis_index("cp")
    x, h = cp // 2, cp % 2
    y_lo, z, core = dp // 8, (dp // 2) % 4, dp % 2
    meta = jnp.stack([x, h, z, core, y_lo]).astype(jnp.int32)
    both = ("dp", "cp")
    half = GROUP // 2

    turned = [lax.ppermute(out_weight, both, x_to_z_pairs(dy)) for dy in (0, 1)]
    (packed,) = call(
        pack_kernel,
        "pack",
        meta,
        (queries, key_heads, value_heads, segment_ids),
        [shaped((8, PACK, ROWS), BF16)],
        [pltpu.SemaphoreType.DMA((8, 5))],
        hbm=(0, 1, 2),
        vmem=60,
    )
    blocks = lax.all_to_all(packed, "cp", 0, 0)
    turned, grad_out = call(
        stack_kernel,
        "turned",
        meta,
        (*turned, grad_out),
        [shaped((2, 192, FEAT), BF16), shaped((GROUP, FEAT), BF16)],
        [pltpu.SemaphoreType.DMA],
        span=20,
        after=(packed,),
        hbm=(2,),
    )
    from_left = lax.ppermute(grad_out, "cp", cp_pairs(1, 0))
    from_right = lax.ppermute(grad_out, "cp", cp_pairs(3, 0))
    weight = lax.all_gather(
        turned, "dp", axis=0, axis_index_groups=[list(range(8)), list(range(8, 16))]
    ).reshape(NX, 2, 2, 192, FEAT)

    wide_scratch = [pltpu.VMEM((HEADS, GROUP, 2 * HD), BF16), pltpu.VMEM((GROUP, 2 * HD), BF16)]
    att_low, q_all, kv_all, v_turned, boundary, stat_low = call(
        forward_low_kernel,
        "forward_low",
        meta,
        (blocks,),
        [
            shaped((half, FEAT), BF16),
            shaped((HEADS, GROUP, HD), BF16),
            shaped((2, GROUP, HD), BF16),
            shaped((HD, GROUP), BF16),
            shaped((8, 128), jnp.int32),
            shaped((8, half), F32),
        ],
        wide_scratch,
        span=0,
    )
    there_low = lax.ppermute(att_low, "cp", cp_pairs(0, 1))
    att_high, stat_high = call(
        forward_high_kernel,
        "forward_high",
        meta,
        (q_all, kv_all, v_turned, boundary),
        [shaped((half, FEAT), BF16), shaped((8, half), F32)],
        wide_scratch,
        span=100,
    )
    there_high = lax.ppermute(att_high, "cp", cp_pairs(0, 1))

    left_low, right_high = call(
        halves_kernel,
        "halves",
        meta,
        (from_left, from_right),
        [shaped((half, FEAT), BF16)] * 2,
        [pltpu.SemaphoreType.DMA((2,))],
        after=(att_high,),
        hbm=(0, 1),
    )
    low = lax.ppermute(left_low, "cp", cp_pairs(1, 0))
    high = lax.ppermute(right_high, "cp", cp_pairs(3, 0))
    grads_out = (grad_out, from_left, from_right, low, high)

    weight_block = whole_block((NX, 2, 2, 192, FEAT))
    (out_all,) = call(
        out_kernel,
        "out",
        meta,
        (att_low, att_high, there_low, there_high, weight),
        [shaped((NX, GROUP, FEAT), BF16)],
        [pltpu.VMEM((2 * FEAT, NX * FEAT), BF16)],
        span=20,
        vmem=61,
        grid=(4,),
        blocks=[row_block(QB, FEAT, lambda i: i % 2)] * 4 + [weight_block],
        out_blocks=[pl.BlockSpec((NX, QB, FEAT), lambda i: (0, i, 0))],
    )
    output = lax.psum_scatter(
        out_all,
        "cp",
        scatter_dimension=0,
        axis_index_groups=[[x * 2 + h for x in range(NX)] for h in range(2)],
    )

    grad_send, grad_own = call(
        grad_kernel,
        "grad_attended",
        meta,
        (*grads_out, weight),
        [shaped((GROUP, FEAT), BF16), shaped((GROUP, FEAT), F32)],
        [pltpu.VMEM((QB, NX * FEAT), BF16), pltpu.VMEM((2 * FEAT, NX * FEAT), BF16)],
        after=(out_all,),
        vmem=61,
        grid=(4,),
        blocks=[row_block(QB, FEAT, lambda i: i)] * 3
        + [row_block(QB, FEAT, lambda i: lax.min(i, 1)), row_block(QB, FEAT, lambda i: lax.max(i - 2, 0)), weight_block],
        out_blocks=[row_block(QB, FEAT, lambda i: i)] * 2,
    )
    grad_part = lax.ppermute(grad_send, "cp", cp_pairs(0, 1))

    keep, *sends = call(
        grad_weight_kernel,
        "grad_weight",
        meta,
        (att_low, att_high, there_low, there_high, *grads_out),
        [shaped((2, NX, 192, FEAT), F32)] + [shaped((NX, 96, FEAT), BF16)] * 4,
        [pltpu.VMEM((GROUP, NX * FEAT), BF16), pltpu.VMEM((FEAT, NX * FEAT), F32)],
        after=(grad_own,),
        span=80,
    )
    core_parts = [lax.ppermute(p, "dp", core_pairs()) for p in sends]

    z_own, *z_sends = call(
        z_kernel,
        "z_sum",
        meta,
        (keep, *core_parts),
        [shaped((2, 192, FEAT), F32)] + [shaped((2, 192, FEAT), BF16)] * 3,
    )
    z_parts = [lax.ppermute(p, "dp", z_pairs(dz)) for dz, p in zip((1, 2, 3), z_sends)]

    (grads,) = call(
        backward_kernel,
        "backward",
        meta,
        (q_all, kv_all, boundary, stat_low, stat_high, grad_own, grad_part),
        [shaped((8, 5 * ROWS, ROWS), BF16)],
        [
            pltpu.VMEM((HD, GROUP), BF16),
            pltpu.VMEM((HEADS, GROUP, HD), BF16),
            pltpu.VMEM((HEADS, GROUP, HD), BF16),
            pltpu.VMEM((GROUP, HD), F32),
            pltpu.VMEM((GROUP, HD), F32),
        ]
        + wide_scratch,
        after=(z_own,),
    )
    returned = lax.all_to_all(grads, "cp", 0, 0)

    y_own, y_send = call(
        y_kernel,
        "y_sum",
        meta,
        (z_own, *z_parts),
        [shaped((192, FEAT), BF16), shaped((192, FEAT), BF16)],
        after=(grads,),
        span=15,
    )
    totals = [lax.ppermute(p, both, x_to_z_pairs(dy)) for dy, p in ((0, y_own), (1, y_send))]
    (grad_weight,) = call(sum_kernel, "grad_weight_total", meta, totals, [shaped((192, FEAT), F32)])

    grad_queries, grad_keys, grad_values = call(
        unpack_kernel,
        "unpack",
        meta,
        (returned,),
        [shaped((ROWS, 8 * FEAT), BF16), shaped((ROWS, 4 * HD), BF16), shaped((ROWS, 4 * HD), BF16)],
    )
    return output, grad_queries, grad_keys, grad_values, grad_weight


def solution(mesh):
    in_specs = (
        P(("dp", "cp"), None),
        P(("dp", "cp"), None),
        P(("dp", "cp"), None),
        P("dp", "cp"),
        P("dp", "cp"),
        P("dp", "cp"),
    )
    out_specs = (
        P("dp", "cp"),
        P(("dp", "cp"), None),
        P(("dp", "cp"), None),
        P(("dp", "cp"), None),
        P("dp", "cp"),
    )
    return jax.shard_map(
        per_device, mesh=mesh, in_specs=in_specs, out_specs=out_specs, check_vma=False
    )
```

```python
import math

import jax
import jax.numpy as jnp
from jax import lax
from jax.experimental import pallas as pl
from jax.experimental.pallas import tpu as pltpu
from jax.sharding import PartitionSpec as P


NX = 4
GROUP = 1024
HD = 128
HEADS = 3
FEAT = 384
ROWS = 128
QB = 256
SEG_ROWS = 16
PACK = 5 * ROWS + SEG_ROWS
SCALE = 1.0 / math.sqrt(HD)
FAR = -(2.0**17)
EXP2_SCALE = SCALE * math.log2(math.e)
F32 = jnp.float32
BF16 = jnp.bfloat16


def cp_pairs(dx, dh):
    return [(x * 2 + h, ((x + dx) % NX) * 2 + (h ^ dh)) for x in range(NX) for h in range(2)]


def z_pairs(dz):
    return [
        (y * 8 + z * 2 + c, y * 8 + ((z + dz) % 4) * 2 + c)
        for y in range(2)
        for z in range(4)
        for c in range(2)
    ]


def core_pairs():
    return [(d, d ^ 1) for d in range(16)]


def x_to_z_pairs(dy):
    return [
        (((y * 4 + z) * 2 + c) * 8 + x * 2 + h, (((y ^ dy) * 4 + x) * 2 + c) * 8 + z * 2 + h)
        for y in range(2)
        for z in range(4)
        for c in range(2)
        for x in range(4)
        for h in range(2)
    ]


def dot_nt(a, b):
    return lax.dot_general(a, b, (((1,), (1,)), ((), ())), preferred_element_type=F32)


def dot_nn(a, b):
    return lax.dot_general(a, b, (((1,), (0,)), ((), ())), preferred_element_type=F32)


def dot_tn(a, b):
    return lax.dot_general(a, b, (((0,), (0,)), ((), ())), preferred_element_type=F32)


def call(
    kernel, name, meta, operands, outs, scratch=(), span=0, after=(), hbm=(), vmem=32, grid=(), blocks=None, out_blocks=None
):
    count = len(operands)

    lead = 0 if meta is None else 1

    def body(*refs):
        head, refs = refs[:lead], refs[lead:]
        kernel(*head, *refs[:count], *refs[count + len(after) :])

    def whole(i):
        return pl.BlockSpec(memory_space=pl.ANY if i in hbm else pltpu.VMEM)

    return pl.pallas_call(
        body,
        name=name,
        out_shape=tuple(outs),
        grid=grid,
        in_specs=[pl.BlockSpec(memory_space=pltpu.SMEM)] * lead
        + (blocks or [whole(i) for i in range(count)])
        + [pl.BlockSpec(memory_space=pl.ANY)] * len(after),
        out_specs=tuple(out_blocks or [pl.BlockSpec(memory_space=pltpu.VMEM) for _ in outs]),
        scratch_shapes=list(scratch),
        compiler_params=pltpu.CompilerParams(vmem_limit_bytes=vmem * 1024 * 1024),
        cost_estimate=pl.CostEstimate(flops=span * 10**9, bytes_accessed=0, transcendentals=0),
    )(*([meta] * lead), *operands, *after)


def row_block(height, width, index):
    return pl.BlockSpec((height, width), lambda i: (index(i), 0))


def whole_block(shape):
    return pl.BlockSpec(shape, lambda i: (0,) * len(shape))


def shaped(shape, dtype):
    return jax.ShapeDtypeStruct(shape, dtype)


def pack_kernel(q_ref, k_ref, v_ref, seg_ref, out, sems):
    copies = []
    for to in range(8):
        to_x, to_h = to // 2, to % 2
        q_off = (to_h * NX + to_x) * FEAT
        kv_off = (to_h * 2 + to_x // 2) * HD
        sources = [q_ref.at[:, pl.ds(q_off + head * HD, HD)] for head in range(HEADS)]
        sources += [k_ref.at[:, pl.ds(kv_off, HD)], v_ref.at[:, pl.ds(kv_off, HD)]]
        for i, source in enumerate(sources):
            copies.append(
                pltpu.make_async_copy(source, out.at[to, pl.ds(i * ROWS, ROWS), :], sems.at[to, i])
            )
            copies[-1].start()
    seg = jnp.broadcast_to(seg_ref[...].astype(F32), (SEG_ROWS, ROWS)).astype(BF16)
    for to in range(8):
        out[to, pl.ds(5 * ROWS, SEG_ROWS), :] = seg
    for copy in copies:
        copy.wait()


def key_parts(qb):
    start = QB if qb == 3 else 0
    return [r for r in ((start, qb * QB, False), (qb * QB, (qb + 1) * QB, True)) if r[0] < r[1]]


def widen(boundary, q_ref, k_ref, q_wide, k_wide):
    shape = (GROUP, HD)
    column = lax.broadcasted_iota(jnp.int32, shape, 1) == 0
    second = lax.broadcasted_iota(jnp.int32, shape, 0) >= boundary
    q_more = jnp.where(column & second, FAR, 0.0).astype(BF16)
    k_more = jnp.where(column & jnp.logical_not(second), 1.0, 0.0).astype(BF16)
    for head in range(HEADS):
        q_wide[head, :, pl.ds(0, HD)] = q_ref[head]
        q_wide[head, :, pl.ds(HD, HD)] = q_more
    k_wide[:, pl.ds(0, HD)] = k_ref[0]
    k_wide[:, pl.ds(HD, HD)] = k_more


def transposed_scores(k, q, diagonal):
    scores = dot_nt(k, q) * EXP2_SCALE
    if diagonal:
        key_pos = lax.broadcasted_iota(jnp.int32, scores.shape, 0)
        query_pos = lax.broadcasted_iota(jnp.int32, scores.shape, 1)
        scores = jnp.where(key_pos <= query_pos, scores, -1e30)
    return scores


def forward_rows(qbs, q_wide, k_wide, vt_ref, att_ref, stat_ref):
    base = qbs[0] * QB
    for qb in qbs:
        out_rows = pl.ds(qb * QB - base, QB)
        for head in range(HEADS):
            q = q_wide[head, pl.ds(qb * QB, QB), :]
            parts = [
                (pl.ds(lo, hi - lo), transposed_scores(k_wide[pl.ds(lo, hi - lo), :], q, diagonal))
                for lo, hi, diagonal in key_parts(qb)
            ]
            peaks = [jnp.max(scores, axis=0, keepdims=True) for _, scores in parts]
            peak = peaks[0] if len(peaks) == 1 else jnp.maximum(*peaks)
            total, mixed = 0.0, 0.0
            for span, scores in parts:
                weights = jnp.exp2(scores - peak)
                total = total + jnp.sum(weights, axis=0, keepdims=True)
                mixed = mixed + dot_nn(vt_ref[:, span], weights.astype(BF16))
            stat_ref[head : head + 1, out_rows] = peak + jnp.log2(total)
            att_ref[out_rows, pl.ds(head * HD, HD)] = (mixed / total).T.astype(BF16)


def forward_low_kernel(
    meta, blocks, att_ref, q_ref, kv_ref, vt_ref, boundary_ref, stat_ref, q_wide, k_wide
):
    seg_sum = jnp.zeros((1, ROWS), F32)
    for source in range(8):
        rows = pl.ds(source * ROWS, ROWS)
        for head in range(HEADS):
            q_ref[head, rows, :] = blocks[source, pl.ds(head * ROWS, ROWS), :]
        kv_ref[0, rows, :] = blocks[source, pl.ds(3 * ROWS, ROWS), :]
        kv_ref[1, rows, :] = blocks[source, pl.ds(4 * ROWS, ROWS), :]
        seg_sum = seg_sum + blocks[source, pl.ds(5 * ROWS, SEG_ROWS), :].astype(F32)[0:1]
    second = jnp.sum(seg_sum, axis=1, keepdims=True)
    boundary = (GROUP - second).astype(jnp.int32)
    boundary_ref[...] = jnp.broadcast_to(boundary, boundary_ref.shape)
    vt_ref[...] = kv_ref[1].astype(F32).T.astype(BF16)
    stat_ref[...] = jnp.zeros_like(stat_ref)
    widen(boundary, q_ref, kv_ref, q_wide, k_wide)
    forward_rows((0, 1), q_wide, k_wide, vt_ref, att_ref, stat_ref)


def forward_high_kernel(meta, q_ref, kv_ref, vt_ref, boundary_ref, att_ref, stat_ref, q_wide, k_wide):
    stat_ref[...] = jnp.zeros_like(stat_ref)
    widen(boundary_ref[0:1, 0:1], q_ref, kv_ref, q_wide, k_wide)
    forward_rows((2, 3), q_wide, k_wide, vt_ref, att_ref, stat_ref)


def backward_kernel(meta, q_ref, kv_ref, boundary_ref, stat_low, stat_high, own_ref, *refs):
    part_ref, out, kt_ref, g_ref, gq_ref, gk_ref, gv_ref, q_wide, k_wide = refs
    total = own_ref[...] + part_ref[...].astype(F32)
    for head in range(HEADS):
        g_ref[head] = total[:, head * HD : (head + 1) * HD].astype(BF16)
    kt_ref[...] = kv_ref[0].astype(F32).T.astype(BF16)
    gk_ref[...] = jnp.zeros_like(gk_ref)
    gv_ref[...] = jnp.zeros_like(gv_ref)
    widen(boundary_ref[0:1, 0:1], q_ref, kv_ref, q_wide, k_wide)
    for qb in range(GROUP // QB):
        rows = pl.ds(qb * QB, QB)
        stat_ref, stat_rows = (stat_low, rows) if qb < 2 else (stat_high, pl.ds(qb * QB - GROUP // 2, QB))
        for head in range(HEADS):
            q = q_ref[head, rows, :]
            g = g_ref[head, rows, :]
            parts, delta = [], 0.0
            for lo, hi, diagonal in key_parts(qb):
                span = pl.ds(lo, hi - lo)
                scores = transposed_scores(k_wide[span, :], q_wide[head, rows, :], diagonal)
                prob = jnp.exp2(scores - stat_ref[head : head + 1, stat_rows])
                grad_prob = dot_nt(kv_ref[1, span, :], g)
                delta = delta + jnp.sum(prob * grad_prob, axis=0, keepdims=True)
                gv_ref[span, :] += dot_nn(prob.astype(BF16), g)
                parts.append((span, prob, grad_prob))
            gq = 0.0
            for span, prob, grad_prob in parts:
                grad_logit = (prob * (grad_prob - delta)).astype(BF16)
                gk_ref[span, :] += dot_nn(grad_logit, q)
                gq = gq + dot_nn(kt_ref[:, span], grad_logit)
            gq_ref[head, rows, :] = (gq * SCALE).T.astype(BF16)
    for to in range(8):
        rows = pl.ds(to * ROWS, ROWS)
        for head in range(HEADS):
            out[to, pl.ds(head * ROWS, ROWS), :] = gq_ref[head, rows, :]
        out[to, pl.ds(3 * ROWS, ROWS), :] = (gk_ref[rows, :] * SCALE).astype(BF16)
        out[to, pl.ds(4 * ROWS, ROWS), :] = gv_ref[rows, :].astype(BF16)


def unpack_kernel(meta, blocks, gq_ref, gk_ref, gv_ref):
    def block(head, first):
        return blocks[(head % NX) * 2 + head // NX, pl.ds(first * ROWS, ROWS), :]

    for source in range(8):
        for head in range(HEADS):
            gq_ref[:, pl.ds(source * FEAT + head * HD, HD)] = block(source, head)
    for head in range(4):
        cols = pl.ds(head * HD, HD)
        for first, out in ((3, gk_ref), (4, gv_ref)):
            both = block(2 * head, first).astype(F32) + block(2 * head + 1, first).astype(F32)
            out[:, cols] = both.astype(BF16)


def gather_columns(x, refs, out):
    own, right, left, low, high = refs
    half = GROUP // 2
    out[:, pl.ds(0, FEAT)] = own[...]
    out[:, pl.ds(FEAT, FEAT)] = right[...]
    out[pl.ds(0, half), pl.ds(2 * FEAT, FEAT)] = low[...]
    out[pl.ds(half, half), pl.ds(2 * FEAT, FEAT)] = high[...]
    out[:, pl.ds(3 * FEAT, FEAT)] = left[...]


def place_weight(meta, w_ref, part, column, out, row, col):
    which = jnp.where(part == meta[4], 0, 1)
    for core in range(2):
        out[pl.ds(row + core * 192, 192), pl.ds(col, FEAT)] = w_ref[column, core, which]


def grad_kernel(meta, *refs):
    grads, w_ref, send_ref, own_ref, held, wide = refs[:5], *refs[5:]
    x, h = meta[0], meta[1]
    step = pl.program_id(0)

    @pl.when(step == 0)
    def _():
        for shift in range(NX):
            slot = lax.rem(x - shift + NX, NX)
            place_weight(meta, w_ref, 1 - h, slot, wide, 0, shift * FEAT)
            place_weight(meta, w_ref, h, slot, wide, FEAT, shift * FEAT)

    own, right, left, low, high = grads
    for shift, part in ((0, own), (1, right), (3, left)):
        held[:, pl.ds(shift * FEAT, FEAT)] = part[...]
    far = pl.ds(2 * FEAT, FEAT)
    is_high = step == 1

    @pl.when(is_high)
    def _():
        held[:, far] = high[...]

    @pl.when(jnp.logical_not(is_high))
    def _():
        held[:, far] = low[...]

    total = dot_nt(held[...], wide[...])
    send_ref[...] = total[:, :FEAT].astype(BF16)
    own_ref[...] = total[:, FEAT:]


def out_kernel(meta, here_low, here_high, there_low, there_high, w_ref, out, wide):
    h = meta[1]
    is_low = pl.program_id(0) == 0

    @pl.when(pl.program_id(0) == 0)
    def _():
        for column in range(NX):
            place_weight(meta, w_ref, h, column, wide, 0, column * FEAT)
            place_weight(meta, w_ref, 1 - h, column, wide, FEAT, column * FEAT)

    here = jnp.where(is_low, here_low[...], here_high[...])
    there = jnp.where(is_low, there_low[...], there_high[...])
    total = dot_nn(here, wide[pl.ds(0, FEAT), :]) + dot_nn(there, wide[pl.ds(FEAT, FEAT), :])
    for column in range(NX):
        out[column] = total[:, column * FEAT : (column + 1) * FEAT].astype(BF16)


def grad_weight_kernel(meta, *refs):
    att, grads, (keep_ref, *sends, held, total) = refs[:4], refs[4:9], refs[9:]
    half = GROUP // 2
    x, h, core = meta[0], meta[1], meta[3]
    gather_columns(x, grads, held)
    for which in range(2):
        part = h if which == 0 else 1 - h
        low, high = att[2 * which][...].T, att[2 * which + 1][...].T
        total[...] = dot_nn(low, held[pl.ds(0, half), :]) + dot_nn(high, held[pl.ds(half, half), :])
        for shift in range(NX):
            slot = lax.rem(x - shift + NX, NX)
            cols = pl.ds(shift * FEAT, FEAT)
            keep_ref[part, slot] = total[pl.ds(pl.multiple_of(core * 192, 64), 192), cols]
            for part_rows in range(2):
                row = pl.multiple_of((1 - core) * 192 + part_rows * 96, 32)
                sends[which * 2 + part_rows][slot] = total[pl.ds(row, 96), cols].astype(BF16)


def z_kernel(meta, keep_ref, *refs):
    parts, own_ref, outs = refs[:4], refs[4], refs[5:]
    h, z = meta[1], meta[2]
    for dz in range(4):
        slot = lax.rem(z + dz, 4)
        for which, row in ((0, h), (1, 1 - h)):
            for part_rows in range(2):
                rows = pl.ds(part_rows * 96, 96)
                total = keep_ref[row, slot, rows, :] + parts[which * 2 + part_rows][slot].astype(F32)
                if dz == 0:
                    own_ref[row, rows, :] = total
                else:
                    outs[dz - 1][row, rows, :] = total.astype(BF16)


def y_kernel(meta, own_ref, *refs):
    parts, (keep_ref, send_ref) = refs[:3], refs[3:]
    y_lo = meta[4]
    for which, out in ((y_lo, keep_ref), (1 - y_lo, send_ref)):
        total = own_ref[which]
        for part in parts:
            total = total + part[which].astype(F32)
        out[...] = total.astype(out.dtype)


def sum_kernel(meta, a_ref, b_ref, out):
    out[...] = a_ref[...].astype(F32) + b_ref[...].astype(F32)


def stack_kernel(meta, a_ref, b_ref, grad_ref, out, grad_out, sem):
    copy = pltpu.make_async_copy(grad_ref, grad_out, sem)
    copy.start()
    out[0] = a_ref[...]
    out[1] = b_ref[...]
    copy.wait()


def halves_kernel(meta, left_ref, right_ref, low_ref, high_ref, sems):
    half = low_ref.shape[0]
    copies = [
        pltpu.make_async_copy(left_ref.at[pl.ds(0, half), :], low_ref, sems.at[0]),
        pltpu.make_async_copy(right_ref.at[pl.ds(half, half), :], high_ref, sems.at[1]),
    ]
    for copy in copies:
        copy.start()
    for copy in copies:
        copy.wait()


def per_device(queries, key_heads, value_heads, segment_ids, out_weight, grad_out):
    dp = lax.axis_index("dp")
    cp = lax.axis_index("cp")
    x, h = cp // 2, cp % 2
    y_lo, z, core = dp // 8, (dp // 2) % 4, dp % 2
    meta = jnp.stack([x, h, z, core, y_lo]).astype(jnp.int32)
    both = ("dp", "cp")
    half = GROUP // 2

    turned = [lax.ppermute(out_weight, both, x_to_z_pairs(dy)) for dy in (0, 1)]
    (packed,) = call(
        pack_kernel,
        "pack",
        None,
        (queries, key_heads, value_heads, segment_ids),
        [shaped((8, PACK, ROWS), BF16)],
        [pltpu.SemaphoreType.DMA((8, 5))],
        hbm=(0, 1, 2),
        vmem=60,
    )
    blocks = lax.all_to_all(packed, "cp", 0, 0)
    turned, grad_out = call(
        stack_kernel,
        "turned",
        meta,
        (*turned, grad_out),
        [shaped((2, 192, FEAT), BF16), shaped((GROUP, FEAT), BF16)],
        [pltpu.SemaphoreType.DMA],
        span=20,
        after=(packed,),
        hbm=(2,),
    )
    from_left = lax.ppermute(grad_out, "cp", cp_pairs(1, 0))
    from_right = lax.ppermute(grad_out, "cp", cp_pairs(3, 0))
    weight = lax.all_gather(
        turned, "dp", axis=0, axis_index_groups=[list(range(8)), list(range(8, 16))]
    ).reshape(NX, 2, 2, 192, FEAT)

    wide_scratch = [pltpu.VMEM((HEADS, GROUP, 2 * HD), BF16), pltpu.VMEM((GROUP, 2 * HD), BF16)]
    att_low, q_all, kv_all, v_turned, boundary, stat_low = call(
        forward_low_kernel,
        "forward_low",
        meta,
        (blocks,),
        [
            shaped((half, FEAT), BF16),
            shaped((HEADS, GROUP, HD), BF16),
            shaped((2, GROUP, HD), BF16),
            shaped((HD, GROUP), BF16),
            shaped((8, 128), jnp.int32),
            shaped((8, half), F32),
        ],
        wide_scratch,
        span=0,
    )
    there_low = lax.ppermute(att_low, "cp", cp_pairs(0, 1))
    att_high, stat_high = call(
        forward_high_kernel,
        "forward_high",
        meta,
        (q_all, kv_all, v_turned, boundary),
        [shaped((half, FEAT), BF16), shaped((8, half), F32)],
        wide_scratch,
        span=100,
    )
    there_high = lax.ppermute(att_high, "cp", cp_pairs(0, 1))

    left_low, right_high = call(
        halves_kernel,
        "halves",
        meta,
        (from_left, from_right),
        [shaped((half, FEAT), BF16)] * 2,
        [pltpu.SemaphoreType.DMA((2,))],
        after=(att_high,),
        hbm=(0, 1),
    )
    low = lax.ppermute(left_low, "cp", cp_pairs(1, 0))
    high = lax.ppermute(right_high, "cp", cp_pairs(3, 0))
    grads_out = (grad_out, from_left, from_right, low, high)

    weight_block = whole_block((NX, 2, 2, 192, FEAT))
    (out_all,) = call(
        out_kernel,
        "out",
        meta,
        (att_low, att_high, there_low, there_high, weight),
        [shaped((NX, GROUP, FEAT), BF16)],
        [pltpu.VMEM((2 * FEAT, NX * FEAT), BF16)],
        span=20,
        vmem=61,
        grid=(2,),
        blocks=[row_block(half, FEAT, lambda i: 0)] * 4 + [weight_block],
        out_blocks=[pl.BlockSpec((NX, half, FEAT), lambda i: (0, i, 0))],
    )
    output = lax.psum_scatter(
        out_all,
        "cp",
        scatter_dimension=0,
        axis_index_groups=[[x * 2 + h for x in range(NX)] for h in range(2)],
    )

    grad_send, grad_own = call(
        grad_kernel,
        "grad_attended",
        meta,
        (*grads_out, weight),
        [shaped((GROUP, FEAT), BF16), shaped((GROUP, FEAT), F32)],
        [pltpu.VMEM((half, NX * FEAT), BF16), pltpu.VMEM((2 * FEAT, NX * FEAT), BF16)],
        after=(out_all,),
        vmem=61,
        grid=(2,),
        blocks=[row_block(half, FEAT, lambda i: i)] * 3
        + [row_block(half, FEAT, lambda i: 0)] * 2
        + [weight_block],
        out_blocks=[row_block(half, FEAT, lambda i: i)] * 2,
    )
    grad_part = lax.ppermute(grad_send, "cp", cp_pairs(0, 1))

    keep, *sends = call(
        grad_weight_kernel,
        "grad_weight",
        meta,
        (att_low, att_high, there_low, there_high, *grads_out),
        [shaped((2, NX, 192, FEAT), F32)] + [shaped((NX, 96, FEAT), BF16)] * 4,
        [pltpu.VMEM((GROUP, NX * FEAT), BF16), pltpu.VMEM((FEAT, NX * FEAT), F32)],
        after=(grad_own,),
        span=80,
    )
    core_parts = [lax.ppermute(p, "dp", core_pairs()) for p in sends]

    z_own, *z_sends = call(
        z_kernel,
        "z_sum",
        meta,
        (keep, *core_parts),
        [shaped((2, 192, FEAT), F32)] + [shaped((2, 192, FEAT), BF16)] * 3,
    )
    z_parts = [lax.ppermute(p, "dp", z_pairs(dz)) for dz, p in zip((1, 2, 3), z_sends)]

    (grads,) = call(
        backward_kernel,
        "backward",
        meta,
        (q_all, kv_all, boundary, stat_low, stat_high, grad_own, grad_part),
        [shaped((8, 5 * ROWS, ROWS), BF16)],
        [
            pltpu.VMEM((HD, GROUP), BF16),
            pltpu.VMEM((HEADS, GROUP, HD), BF16),
            pltpu.VMEM((HEADS, GROUP, HD), BF16),
            pltpu.VMEM((GROUP, HD), F32),
            pltpu.VMEM((GROUP, HD), F32),
        ]
        + wide_scratch,
        after=(z_own,),
    )
    returned = lax.all_to_all(grads, "cp", 0, 0)

    y_own, y_send = call(
        y_kernel,
        "y_sum",
        meta,
        (z_own, *z_parts),
        [shaped((192, FEAT), BF16), shaped((192, FEAT), BF16)],
        after=(grads,),
        span=15,
    )
    totals = [lax.ppermute(p, both, x_to_z_pairs(dy)) for dy, p in ((0, y_own), (1, y_send))]
    (grad_weight,) = call(sum_kernel, "grad_weight_total", meta, totals, [shaped((192, FEAT), F32)])

    grad_queries, grad_keys, grad_values = call(
        unpack_kernel,
        "unpack",
        meta,
        (returned,),
        [shaped((ROWS, 8 * FEAT), BF16), shaped((ROWS, 4 * HD), BF16), shaped((ROWS, 4 * HD), BF16)],
    )
    return output, grad_queries, grad_keys, grad_values, grad_weight


def solution(mesh):
    in_specs = (
        P(("dp", "cp"), None),
        P(("dp", "cp"), None),
        P(("dp", "cp"), None),
        P("dp", "cp"),
        P("dp", "cp"),
        P("dp", "cp"),
    )
    out_specs = (
        P("dp", "cp"),
        P(("dp", "cp"), None),
        P(("dp", "cp"), None),
        P(("dp", "cp"), None),
        P("dp", "cp"),
    )
    return jax.shard_map(
        per_device, mesh=mesh, in_specs=in_specs, out_specs=out_specs, check_vma=False
    )
```

```python
import math

import jax
import jax.numpy as jnp
from jax import lax
from jax.experimental import pallas as pl
from jax.experimental.pallas import tpu as pltpu
from jax.sharding import PartitionSpec as P


NX = 4
GROUP = 1024
HD = 128
HEADS = 3
FEAT = 384
ROWS = 128
QB = 256
SEG_ROWS = 16
PACK = 5 * ROWS + SEG_ROWS
SCALE = 1.0 / math.sqrt(HD)
FAR = -(2.0**17)
EXP2_SCALE = SCALE * math.log2(math.e)
F32 = jnp.float32
BF16 = jnp.bfloat16


def cp_pairs(dx, dh):
    return [(x * 2 + h, ((x + dx) % NX) * 2 + (h ^ dh)) for x in range(NX) for h in range(2)]


def z_pairs(dz):
    return [
        (y * 8 + z * 2 + c, y * 8 + ((z + dz) % 4) * 2 + c)
        for y in range(2)
        for z in range(4)
        for c in range(2)
    ]


def core_pairs():
    return [(d, d ^ 1) for d in range(16)]


def x_to_z_pairs(dy):
    return [
        (((y * 4 + z) * 2 + c) * 8 + x * 2 + h, (((y ^ dy) * 4 + x) * 2 + c) * 8 + z * 2 + h)
        for y in range(2)
        for z in range(4)
        for c in range(2)
        for x in range(4)
        for h in range(2)
    ]


def dot_nt(a, b):
    return lax.dot_general(a, b, (((1,), (1,)), ((), ())), preferred_element_type=F32)


def dot_nn(a, b):
    return lax.dot_general(a, b, (((1,), (0,)), ((), ())), preferred_element_type=F32)


def dot_tn(a, b):
    return lax.dot_general(a, b, (((0,), (0,)), ((), ())), preferred_element_type=F32)


def call(
    kernel, name, meta, operands, outs, scratch=(), span=0, after=(), hbm=(), vmem=32, grid=(), blocks=None, out_blocks=None
):
    count = len(operands)

    lead = 0 if meta is None else 1

    def body(*refs):
        head, refs = refs[:lead], refs[lead:]
        kernel(*head, *refs[:count], *refs[count + len(after) :])

    def whole(i):
        return pl.BlockSpec(memory_space=pl.ANY if i in hbm else pltpu.VMEM)

    return pl.pallas_call(
        body,
        name=name,
        out_shape=tuple(outs),
        grid=grid,
        in_specs=[pl.BlockSpec(memory_space=pltpu.SMEM)] * lead
        + (blocks or [whole(i) for i in range(count)])
        + [pl.BlockSpec(memory_space=pl.ANY)] * len(after),
        out_specs=tuple(out_blocks or [pl.BlockSpec(memory_space=pltpu.VMEM) for _ in outs]),
        scratch_shapes=list(scratch),
        compiler_params=pltpu.CompilerParams(vmem_limit_bytes=vmem * 1024 * 1024),
        cost_estimate=pl.CostEstimate(flops=span * 10**9, bytes_accessed=0, transcendentals=0),
    )(*([meta] * lead), *operands, *after)


def row_block(height, width, index):
    return pl.BlockSpec((height, width), lambda i: (index(i), 0))


def whole_block(shape):
    return pl.BlockSpec(shape, lambda i: (0,) * len(shape))


def shaped(shape, dtype):
    return jax.ShapeDtypeStruct(shape, dtype)


def pack_kernel(q_ref, k_ref, v_ref, seg_ref, out, sems):
    copies = []
    for to in range(8):
        to_x, to_h = to // 2, to % 2
        q_off = (to_h * NX + to_x) * FEAT
        kv_off = (to_h * 2 + to_x // 2) * HD
        sources = [q_ref.at[:, pl.ds(q_off + head * HD, HD)] for head in range(HEADS)]
        sources += [k_ref.at[:, pl.ds(kv_off, HD)], v_ref.at[:, pl.ds(kv_off, HD)]]
        for i, source in enumerate(sources):
            copies.append(
                pltpu.make_async_copy(source, out.at[to, pl.ds(i * ROWS, ROWS), :], sems.at[to, i])
            )
            copies[-1].start()
    seg = jnp.broadcast_to(seg_ref[...].astype(F32), (SEG_ROWS, ROWS)).astype(BF16)
    for to in range(8):
        out[to, pl.ds(5 * ROWS, SEG_ROWS), :] = seg
    for copy in copies:
        copy.wait()


def key_parts(qb):
    start = QB if qb == 3 else 0
    return [r for r in ((start, qb * QB, False), (qb * QB, (qb + 1) * QB, True)) if r[0] < r[1]]


def widen(boundary, q_ref, k_ref, q_wide, k_wide):
    shape = (GROUP, HD)
    column = lax.broadcasted_iota(jnp.int32, shape, 1) == 0
    second = lax.broadcasted_iota(jnp.int32, shape, 0) >= boundary
    q_more = jnp.where(column & second, FAR, 0.0).astype(BF16)
    k_more = jnp.where(column & jnp.logical_not(second), 1.0, 0.0).astype(BF16)
    for head in range(HEADS):
        q_wide[head, :, pl.ds(0, HD)] = q_ref[head]
        q_wide[head, :, pl.ds(HD, HD)] = q_more
    k_wide[:, pl.ds(0, HD)] = k_ref[0]
    k_wide[:, pl.ds(HD, HD)] = k_more


def transposed_scores(k, q, diagonal):
    scores = dot_nt(k, q) * EXP2_SCALE
    if diagonal:
        key_pos = lax.broadcasted_iota(jnp.int32, scores.shape, 0)
        query_pos = lax.broadcasted_iota(jnp.int32, scores.shape, 1) % QB
        scores = jnp.where(key_pos <= query_pos, scores, -1e30)
    return scores


def forward_rows(qbs, q_wide, k_wide, vt_ref, att_ref, stat_ref):
    base = qbs[0] * QB
    for qb in qbs:
        out_rows = pl.ds(qb * QB - base, QB)
        for head in range(HEADS):
            q = q_wide[head, pl.ds(qb * QB, QB), :]
            parts = [
                (pl.ds(lo, hi - lo), transposed_scores(k_wide[pl.ds(lo, hi - lo), :], q, diagonal))
                for lo, hi, diagonal in key_parts(qb)
            ]
            peaks = [jnp.max(scores, axis=0, keepdims=True) for _, scores in parts]
            peak = peaks[0] if len(peaks) == 1 else jnp.maximum(*peaks)
            total, mixed = 0.0, 0.0
            for span, scores in parts:
                weights = jnp.exp2(scores - peak)
                total = total + jnp.sum(weights, axis=0, keepdims=True)
                mixed = mixed + dot_nn(vt_ref[:, span], weights.astype(BF16))
            stat_ref[head : head + 1, out_rows] = peak + jnp.log2(total)
            att_ref[out_rows, pl.ds(head * HD, HD)] = (mixed / total).T.astype(BF16)


def forward_low_kernel(
    meta, blocks, att_ref, q_ref, kv_ref, vt_ref, boundary_ref, stat_ref, q_wide, k_wide
):
    seg_sum = jnp.zeros((1, ROWS), F32)
    for source in range(8):
        rows = pl.ds(source * ROWS, ROWS)
        for head in range(HEADS):
            q_ref[head, rows, :] = blocks[source, pl.ds(head * ROWS, ROWS), :]
        kv_ref[0, rows, :] = blocks[source, pl.ds(3 * ROWS, ROWS), :]
        kv_ref[1, rows, :] = blocks[source, pl.ds(4 * ROWS, ROWS), :]
        seg_sum = seg_sum + blocks[source, pl.ds(5 * ROWS, SEG_ROWS), :].astype(F32)[0:1]
    second = jnp.sum(seg_sum, axis=1, keepdims=True)
    boundary = (GROUP - second).astype(jnp.int32)
    boundary_ref[...] = jnp.broadcast_to(boundary, boundary_ref.shape)
    vt_ref[...] = kv_ref[1].astype(F32).T.astype(BF16)
    stat_ref[...] = jnp.zeros_like(stat_ref)
    widen(boundary, q_ref, kv_ref, q_wide, k_wide)
    forward_rows((0, 1), q_wide, k_wide, vt_ref, att_ref, stat_ref)


def forward_high_kernel(meta, q_ref, kv_ref, vt_ref, boundary_ref, att_ref, stat_ref, q_wide, k_wide):
    stat_ref[...] = jnp.zeros_like(stat_ref)
    widen(boundary_ref[0:1, 0:1], q_ref, kv_ref, q_wide, k_wide)
    forward_rows((2, 3), q_wide, k_wide, vt_ref, att_ref, stat_ref)


def backward_kernel(meta, q_ref, kv_ref, boundary_ref, stat_low, stat_high, own_ref, *refs):
    part_ref, out, kt_ref, g_ref, gq_ref, gk_ref, gv_ref, q_wide, k_wide = refs
    total = own_ref[...] + part_ref[...].astype(F32)
    for head in range(HEADS):
        g_ref[head] = total[:, head * HD : (head + 1) * HD].astype(BF16)
    kt_ref[...] = kv_ref[0].astype(F32).T.astype(BF16)
    gk_ref[...] = jnp.zeros_like(gk_ref)
    gv_ref[...] = jnp.zeros_like(gv_ref)
    widen(boundary_ref[0:1, 0:1], q_ref, kv_ref, q_wide, k_wide)
    for qb in range(GROUP // QB):
        rows = pl.ds(qb * QB, QB)
        stat_ref, stat_rows = (stat_low, rows) if qb < 2 else (stat_high, pl.ds(qb * QB - GROUP // 2, QB))
        q = q_ref[:, rows, :].reshape(HEADS * QB, HD)
        g = g_ref[:, rows, :].reshape(HEADS * QB, HD)
        q_more = q_wide[:, rows, :].reshape(HEADS * QB, 2 * HD)
        stat = jnp.concatenate([stat_ref[head : head + 1, stat_rows] for head in range(HEADS)], axis=1)
        parts, delta = [], 0.0
        for lo, hi, diagonal in key_parts(qb):
            span = pl.ds(lo, hi - lo)
            prob = jnp.exp2(transposed_scores(k_wide[span, :], q_more, diagonal) - stat)
            grad_prob = dot_nt(kv_ref[1, span, :], g)
            delta = delta + jnp.sum(prob * grad_prob, axis=0, keepdims=True)
            gv_ref[span, :] += dot_nn(prob.astype(BF16), g)
            parts.append((span, prob, grad_prob))
        gq = 0.0
        for span, prob, grad_prob in parts:
            grad_logit = (prob * (grad_prob - delta)).astype(BF16)
            gk_ref[span, :] += dot_nn(grad_logit, q)
            gq = gq + dot_nn(kt_ref[:, span], grad_logit)
        gq_ref[:, rows, :] = (gq * SCALE).T.astype(BF16).reshape(HEADS, QB, HD)
    for to in range(8):
        rows = pl.ds(to * ROWS, ROWS)
        for head in range(HEADS):
            out[to, pl.ds(head * ROWS, ROWS), :] = gq_ref[head, rows, :]
        out[to, pl.ds(3 * ROWS, ROWS), :] = (gk_ref[rows, :] * SCALE).astype(BF16)
        out[to, pl.ds(4 * ROWS, ROWS), :] = gv_ref[rows, :].astype(BF16)


def unpack_kernel(meta, blocks, gq_ref, gk_ref, gv_ref):
    def block(head, first):
        return blocks[(head % NX) * 2 + head // NX, pl.ds(first * ROWS, ROWS), :]

    for source in range(8):
        for head in range(HEADS):
            gq_ref[:, pl.ds(source * FEAT + head * HD, HD)] = block(source, head)
    for head in range(4):
        cols = pl.ds(head * HD, HD)
        for first, out in ((3, gk_ref), (4, gv_ref)):
            both = block(2 * head, first).astype(F32) + block(2 * head + 1, first).astype(F32)
            out[:, cols] = both.astype(BF16)


def gather_columns(x, refs, out):
    own, right, left, low, high = refs
    half = GROUP // 2
    out[:, pl.ds(0, FEAT)] = own[...]
    out[:, pl.ds(FEAT, FEAT)] = right[...]
    out[pl.ds(0, half), pl.ds(2 * FEAT, FEAT)] = low[...]
    out[pl.ds(half, half), pl.ds(2 * FEAT, FEAT)] = high[...]
    out[:, pl.ds(3 * FEAT, FEAT)] = left[...]


def place_weight(meta, w_ref, part, column, out, row, col):
    which = jnp.where(part == meta[4], 0, 1)
    for core in range(2):
        out[pl.ds(row + core * 192, 192), pl.ds(col, FEAT)] = w_ref[column, core, which]


def grad_kernel(meta, *refs):
    grads, w_ref, send_ref, own_ref, held, wide = refs[:5], *refs[5:]
    x, h = meta[0], meta[1]
    step = pl.program_id(0)

    @pl.when(step == 0)
    def _():
        for shift in range(NX):
            slot = lax.rem(x - shift + NX, NX)
            place_weight(meta, w_ref, 1 - h, slot, wide, 0, shift * FEAT)
            place_weight(meta, w_ref, h, slot, wide, FEAT, shift * FEAT)

    own, right, left, low, high = grads
    for shift, part in ((0, own), (1, right), (3, left)):
        held[:, pl.ds(shift * FEAT, FEAT)] = part[...]
    far = pl.ds(2 * FEAT, FEAT)
    is_high = step == 1

    @pl.when(is_high)
    def _():
        held[:, far] = high[...]

    @pl.when(jnp.logical_not(is_high))
    def _():
        held[:, far] = low[...]

    total = dot_nt(held[...], wide[...])
    send_ref[...] = total[:, :FEAT].astype(BF16)
    own_ref[...] = total[:, FEAT:]


def out_kernel(meta, here_low, here_high, there_low, there_high, w_ref, out, wide):
    h = meta[1]
    is_low = pl.program_id(0) == 0

    @pl.when(pl.program_id(0) == 0)
    def _():
        for column in range(NX):
            place_weight(meta, w_ref, h, column, wide, 0, column * FEAT)
            place_weight(meta, w_ref, 1 - h, column, wide, FEAT, column * FEAT)

    here = jnp.where(is_low, here_low[...], here_high[...])
    there = jnp.where(is_low, there_low[...], there_high[...])
    total = dot_nn(here, wide[pl.ds(0, FEAT), :]) + dot_nn(there, wide[pl.ds(FEAT, FEAT), :])
    for column in range(NX):
        out[column] = total[:, column * FEAT : (column + 1) * FEAT].astype(BF16)


def grad_weight_kernel(meta, *refs):
    att, grads, (keep_ref, *sends, held, total) = refs[:4], refs[4:9], refs[9:]
    half = GROUP // 2
    x, h, core = meta[0], meta[1], meta[3]
    gather_columns(x, grads, held)
    for which in range(2):
        part = h if which == 0 else 1 - h
        low, high = att[2 * which][...].T, att[2 * which + 1][...].T
        total[...] = dot_nn(low, held[pl.ds(0, half), :]) + dot_nn(high, held[pl.ds(half, half), :])
        for shift in range(NX):
            slot = lax.rem(x - shift + NX, NX)
            cols = pl.ds(shift * FEAT, FEAT)
            keep_ref[part, slot] = total[pl.ds(pl.multiple_of(core * 192, 64), 192), cols]
            for part_rows in range(2):
                row = pl.multiple_of((1 - core) * 192 + part_rows * 96, 32)
                sends[which * 2 + part_rows][slot] = total[pl.ds(row, 96), cols].astype(BF16)


def z_kernel(meta, keep_ref, *refs):
    parts, own_ref, outs = refs[:4], refs[4], refs[5:]
    h, z = meta[1], meta[2]
    for dz in range(4):
        slot = lax.rem(z + dz, 4)
        for which, row in ((0, h), (1, 1 - h)):
            for part_rows in range(2):
                rows = pl.ds(part_rows * 96, 96)
                total = keep_ref[row, slot, rows, :] + parts[which * 2 + part_rows][slot].astype(F32)
                if dz == 0:
                    own_ref[row, rows, :] = total
                else:
                    outs[dz - 1][row, rows, :] = total.astype(BF16)


def y_kernel(meta, own_ref, *refs):
    parts, (keep_ref, send_ref) = refs[:3], refs[3:]
    y_lo = meta[4]
    for which, out in ((y_lo, keep_ref), (1 - y_lo, send_ref)):
        total = own_ref[which]
        for part in parts:
            total = total + part[which].astype(F32)
        out[...] = total.astype(out.dtype)


def sum_kernel(meta, a_ref, b_ref, out):
    out[...] = a_ref[...].astype(F32) + b_ref[...].astype(F32)


def stack_kernel(meta, a_ref, b_ref, grad_ref, out, grad_out, sem):
    copy = pltpu.make_async_copy(grad_ref, grad_out, sem)
    copy.start()
    out[0] = a_ref[...]
    out[1] = b_ref[...]
    copy.wait()


def halves_kernel(meta, left_ref, right_ref, low_ref, high_ref, sems):
    half = low_ref.shape[0]
    copies = [
        pltpu.make_async_copy(left_ref.at[pl.ds(0, half), :], low_ref, sems.at[0]),
        pltpu.make_async_copy(right_ref.at[pl.ds(half, half), :], high_ref, sems.at[1]),
    ]
    for copy in copies:
        copy.start()
    for copy in copies:
        copy.wait()


def per_device(queries, key_heads, value_heads, segment_ids, out_weight, grad_out):
    dp = lax.axis_index("dp")
    cp = lax.axis_index("cp")
    x, h = cp // 2, cp % 2
    y_lo, z, core = dp // 8, (dp // 2) % 4, dp % 2
    meta = jnp.stack([x, h, z, core, y_lo]).astype(jnp.int32)
    both = ("dp", "cp")
    half = GROUP // 2

    turned = [lax.ppermute(out_weight, both, x_to_z_pairs(dy)) for dy in (0, 1)]
    (packed,) = call(
        pack_kernel,
        "pack",
        None,
        (queries, key_heads, value_heads, segment_ids),
        [shaped((8, PACK, ROWS), BF16)],
        [pltpu.SemaphoreType.DMA((8, 5))],
        hbm=(0, 1, 2),
        vmem=60,
    )
    blocks = lax.all_to_all(packed, "cp", 0, 0)
    turned, grad_out = call(
        stack_kernel,
        "turned",
        meta,
        (*turned, grad_out),
        [shaped((2, 192, FEAT), BF16), shaped((GROUP, FEAT), BF16)],
        [pltpu.SemaphoreType.DMA],
        span=20,
        after=(packed,),
        hbm=(2,),
    )
    from_left = lax.ppermute(grad_out, "cp", cp_pairs(1, 0))
    from_right = lax.ppermute(grad_out, "cp", cp_pairs(3, 0))
    weight = lax.all_gather(
        turned, "dp", axis=0, axis_index_groups=[list(range(8)), list(range(8, 16))]
    ).reshape(NX, 2, 2, 192, FEAT)

    wide_scratch = [pltpu.VMEM((HEADS, GROUP, 2 * HD), BF16), pltpu.VMEM((GROUP, 2 * HD), BF16)]
    att_low, q_all, kv_all, v_turned, boundary, stat_low = call(
        forward_low_kernel,
        "forward_low",
        meta,
        (blocks,),
        [
            shaped((half, FEAT), BF16),
            shaped((HEADS, GROUP, HD), BF16),
            shaped((2, GROUP, HD), BF16),
            shaped((HD, GROUP), BF16),
            shaped((8, 128), jnp.int32),
            shaped((8, half), F32),
        ],
        wide_scratch,
        span=0,
    )
    there_low = lax.ppermute(att_low, "cp", cp_pairs(0, 1))
    att_high, stat_high = call(
        forward_high_kernel,
        "forward_high",
        meta,
        (q_all, kv_all, v_turned, boundary),
        [shaped((half, FEAT), BF16), shaped((8, half), F32)],
        wide_scratch,
        span=100,
    )
    there_high = lax.ppermute(att_high, "cp", cp_pairs(0, 1))

    left_low, right_high = call(
        halves_kernel,
        "halves",
        meta,
        (from_left, from_right),
        [shaped((half, FEAT), BF16)] * 2,
        [pltpu.SemaphoreType.DMA((2,))],
        after=(att_high,),
        hbm=(0, 1),
    )
    low = lax.ppermute(left_low, "cp", cp_pairs(1, 0))
    high = lax.ppermute(right_high, "cp", cp_pairs(3, 0))
    grads_out = (grad_out, from_left, from_right, low, high)

    weight_block = whole_block((NX, 2, 2, 192, FEAT))
    (out_all,) = call(
        out_kernel,
        "out",
        meta,
        (att_low, att_high, there_low, there_high, weight),
        [shaped((NX, GROUP, FEAT), BF16)],
        [pltpu.VMEM((2 * FEAT, NX * FEAT), BF16)],
        span=20,
        vmem=61,
        grid=(2,),
        blocks=[row_block(half, FEAT, lambda i: 0)] * 4 + [weight_block],
        out_blocks=[pl.BlockSpec((NX, half, FEAT), lambda i: (0, i, 0))],
    )
    output = lax.psum_scatter(
        out_all,
        "cp",
        scatter_dimension=0,
        axis_index_groups=[[x * 2 + h for x in range(NX)] for h in range(2)],
    )

    grad_send, grad_own = call(
        grad_kernel,
        "grad_attended",
        meta,
        (*grads_out, weight),
        [shaped((GROUP, FEAT), BF16), shaped((GROUP, FEAT), F32)],
        [pltpu.VMEM((half, NX * FEAT), BF16), pltpu.VMEM((2 * FEAT, NX * FEAT), BF16)],
        after=(out_all,),
        vmem=61,
        grid=(2,),
        blocks=[row_block(half, FEAT, lambda i: i)] * 3
        + [row_block(half, FEAT, lambda i: 0)] * 2
        + [weight_block],
        out_blocks=[row_block(half, FEAT, lambda i: i)] * 2,
    )
    grad_part = lax.ppermute(grad_send, "cp", cp_pairs(0, 1))

    keep, *sends = call(
        grad_weight_kernel,
        "grad_weight",
        meta,
        (att_low, att_high, there_low, there_high, *grads_out),
        [shaped((2, NX, 192, FEAT), F32)] + [shaped((NX, 96, FEAT), BF16)] * 4,
        [pltpu.VMEM((GROUP, NX * FEAT), BF16), pltpu.VMEM((FEAT, NX * FEAT), F32)],
        after=(grad_own,),
        span=80,
    )
    core_parts = [lax.ppermute(p, "dp", core_pairs()) for p in sends]

    z_own, *z_sends = call(
        z_kernel,
        "z_sum",
        meta,
        (keep, *core_parts),
        [shaped((2, 192, FEAT), F32)] + [shaped((2, 192, FEAT), BF16)] * 3,
    )
    z_parts = [lax.ppermute(p, "dp", z_pairs(dz)) for dz, p in zip((1, 2, 3), z_sends)]

    (grads,) = call(
        backward_kernel,
        "backward",
        meta,
        (q_all, kv_all, boundary, stat_low, stat_high, grad_own, grad_part),
        [shaped((8, 5 * ROWS, ROWS), BF16)],
        [
            pltpu.VMEM((HD, GROUP), BF16),
            pltpu.VMEM((HEADS, GROUP, HD), BF16),
            pltpu.VMEM((HEADS, GROUP, HD), BF16),
            pltpu.VMEM((GROUP, HD), F32),
            pltpu.VMEM((GROUP, HD), F32),
        ]
        + wide_scratch,
        after=(z_own,),
    )
    returned = lax.all_to_all(grads, "cp", 0, 0)

    y_own, y_send = call(
        y_kernel,
        "y_sum",
        meta,
        (z_own, *z_parts),
        [shaped((192, FEAT), BF16), shaped((192, FEAT), BF16)],
        after=(grads,),
        span=15,
    )
    totals = [lax.ppermute(p, both, x_to_z_pairs(dy)) for dy, p in ((0, y_own), (1, y_send))]
    (grad_weight,) = call(sum_kernel, "grad_weight_total", meta, totals, [shaped((192, FEAT), F32)])

    grad_queries, grad_keys, grad_values = call(
        unpack_kernel,
        "unpack",
        meta,
        (returned,),
        [shaped((ROWS, 8 * FEAT), BF16), shaped((ROWS, 4 * HD), BF16), shaped((ROWS, 4 * HD), BF16)],
    )
    return output, grad_queries, grad_keys, grad_values, grad_weight


def solution(mesh):
    in_specs = (
        P(("dp", "cp"), None),
        P(("dp", "cp"), None),
        P(("dp", "cp"), None),
        P("dp", "cp"),
        P("dp", "cp"),
        P("dp", "cp"),
    )
    out_specs = (
        P("dp", "cp"),
        P(("dp", "cp"), None),
        P(("dp", "cp"), None),
        P(("dp", "cp"), None),
        P("dp", "cp"),
    )
    return jax.shard_map(
        per_device, mesh=mesh, in_specs=in_specs, out_specs=out_specs, check_vma=False
    )
```
